32 devices in a mesh: dp: 16 (over z, x, core), mp: 2 (over y).
Axes of the slice: x: 2, y: 2, z: 4, core: 2. Of those that a mesh axis runs over, the one named last changes fastest.
Arguments:
- tokens: bfloat16 [8192, 768], P('dp'), may hold values from -6 to 6
- gain_attn: bfloat16 [768], replicated, may hold values from 0.5 to 1.5
- w_query: bfloat16 [768, 768], P(None, 'mp'), may hold values from -0.0546875 to 0.0546875
- w_key: bfloat16 [768, 768], P(None, 'mp'), may hold values from -0.21875 to 0.21875
- w_value: bfloat16 [768, 768], P(None, 'mp'), may hold values from -0.21875 to 0.21875
- w_output: bfloat16 [768, 768], P('mp'), may hold values from -0.625 to 0.625
- position_table: bfloat16 [32, 12], P(None, 'mp'), may hold values from -5 to 5
- gain_moe: bfloat16 [768], replicated, may hold values from 0.5 to 1.5
- w_router: bfloat16 [768, 4], replicated, may hold values from -0.15625 to 0.15625
- w_in: bfloat16 [4, 768, 3072], P(None, None, 'mp'), may hold values from -0.21875 to 0.21875
- w_out: bfloat16 [4, 3072, 768], P(None, 'mp'), may hold values from -1.5 to 1.5
- cotangent: bfloat16 [8192, 768], P('dp'), may hold values from -6 to 6
- seq_lengths: int32 [16, 4], P('dp'), may hold values from 0 to 512, as said below
- expert_ids: int32 [8192], P('dp'), may hold values from 0 to 3, as said below
Outputs:
- mixed: bfloat16 [8192, 768], P('dp')
- grad_tokens: float32 [8192, 768], P('dp')
- grad_gain_attn: float32 [768], P('dp')
- grad_query: float32 [768, 768], P('dp', 'mp')
- grad_key: float32 [768, 768], P('dp', 'mp')
- grad_value: float32 [768, 768], P('dp', 'mp')
- grad_output: float32 [768, 768], P('mp', 'dp')
- grad_table: float32 [32, 12], P(None, 'mp')
- grad_gain_moe: float32 [768], P('dp')
- grad_router: float32 [768, 4], P('dp')
- grad_in: float32 [4, 768, 3072], P(None, 'dp', 'mp')
- grad_out: float32 [4, 3072, 768], P(None, 'mp', 'dp')
The draws below stay inside these ranges and needn't reach their ends.
Inputs may be any that keep to these rules, and one draw needn't show every extreme that they name: `seq_lengths`: row b lists the lengths of the sequences that fill token batch b from its first slot on, in order, 0 for an unused entry; a row sums to 512 or less, the slots after it being padding; in every draw some row is one sequence of 512 tokens. `expert_ids`: in every token batch some expert is named by at least 160 of its 512 tokens.
All inputs are finite; a program needn't handle non-finite values.
Results may differ from the reference program's by a relative error of at most 0.017.
The reference program's roundings to bfloat16 on the way count: a program that leaves them out, or rounds other values in their place, can miss the bound.
Values sent between devices are 32-bit elements; how exact they have to be, the bound alone decides.
No kernel may reach another device: no remote copies, remote signals or barrier semaphores. Data moves between devices by JAX's collectives and lax.ppermute only.
A program may use at most 192 MiB of HBM per device.

```python
import jax
import jax.numpy as jnp
from jax import lax

D = 768
HEADS = 12
HEAD = 64
FF = 3072
NB = 32
E = 4
SEQS = 4
TOK_DEV = 512
CAP = 160
HD = 768
TOKENS = 8192
N_DP = 16


def draw_seq_lengths(key, part):
    key = jax.random.fold_in(key, 11)
    first, second, third = jax.random.split(key, 3)
    totals = jax.random.randint(first, (N_DP, 1), TOK_DEV // 2, TOK_DEV + 1)
    cuts = jax.random.randint(second, (N_DP, SEQS - 1), 0, totals + 1)
    cuts = jnp.sort(cuts, axis=1)
    edges = jnp.concatenate([jnp.zeros((N_DP, 1), jnp.int32), cuts.astype(jnp.int32), totals.astype(jnp.int32)], axis=1)
    lengths = edges[:, 1:] - edges[:, :-1]
    whole = jax.random.randint(third, (), 0, N_DP)
    single = jnp.concatenate([jnp.full((1, 1), TOK_DEV, jnp.int32), jnp.zeros((1, SEQS - 1), jnp.int32)], axis=1)
    rows = jnp.arange(N_DP)[:, None]
    return jnp.where(rows == whole, single, lengths).astype(jnp.int32)


def draw_expert_ids(key, part):
    key = jax.random.fold_in(key, 23)
    first, second, third = jax.random.split(key, 3)
    busiest = jax.random.randint(first, (N_DP, 1), 0, E)
    spread = jax.random.randint(second, (N_DP, TOK_DEV), 0, E)
    scores = jax.random.randint(third, (N_DP, TOK_DEV), 0, 2 ** 30)
    order = jnp.argsort(jnp.argsort(scores, axis=1, stable=True), axis=1, stable=True)
    forced = order < CAP
    return jnp.where(forced, busiest, spread).reshape(N_DP * TOK_DEV).astype(jnp.int32)


def spiked(entries, rng, source, target, shards_of, factor):
    def block_of(dim):
        return (jnp.arange(entries.shape[dim]) // (entries.shape[dim] // shards_of)).reshape((-1,) + (1,) * (entries.ndim - 1 - dim))

    one_side = jax.random.permutation(rng, shards_of)[block_of(target)]
    other_side = (block_of(target) + shards_of // 2) % shards_of
    return jnp.where((block_of(source) == one_side) | (block_of(source) == other_side), factor * entries, entries)


def level_of(key, extent, shards, low, largest):
    level, own = 1.0, jax.random.fold_in(key, 6)
    for dim, blocks in shards:
        draws = jnp.exp(jax.random.uniform(jax.random.fold_in(own, dim), (blocks,), jnp.float32, low / len(shards), largest / len(shards)))
        level = level * jnp.repeat(draws, extent[dim] // blocks).reshape([-1 if axis == dim else 1 for axis in range(len(extent))])
    return level


def noise(stream_key, dims, scale, reach, pieces=(), kind=jnp.bfloat16):
    drawn = jax.random.normal(stream_key, dims, jnp.float32) * scale
    if len(pieces) > 0:
        drawn = level_of(stream_key, dims, pieces, -0.22, 0.18) * drawn
    return jnp.clip(drawn, min=-reach, max=reach).astype(kind)


def heavy_noise(key, shape, width, reach, pieces, heavy, kind=jnp.bfloat16):
    entries = width * jax.random.normal(key, shape, jnp.float32)
    if pieces:
        entries = entries * level_of(key, shape, pieces, -0.22, 0.18)
    return jnp.clip(spiked(entries, jax.random.fold_in(key, 3), *heavy), -reach, reach).astype(kind)


def setup_inputs(seed: int = 0) -> dict:
    key_list = jax.random.split(jax.random.key(seed), 15)
    tokens = noise(key_list[0], (TOKENS, D), 1.0, 6.0, ((0, 16),))
    gain_attn = jnp.clip(1.0 + 0.1 * jax.random.normal(key_list[1], (D,), jnp.float32), 0.5, 1.5).astype(jnp.bfloat16)
    w_query = noise(key_list[2], (D, HD), (16 * D) ** -0.5, 0.0546875, ((1, 2),))
    w_key = noise(key_list[3], (D, HD), D ** -0.5, 0.21875, ((1, 2),))
    w_value = noise(key_list[4], (D, HD), D ** -0.5, 0.21875, ((1, 2),))
    w_output = noise(key_list[5], (HD, D), (HD // 8) ** -0.5, 0.625, ((0, 2),))
    position_table = noise(key_list[6], (NB, HEADS), 1.0, 5.0, ((1, 2),))
    gain_moe = jnp.clip(1.0 + 0.1 * jax.random.normal(key_list[7], (D,), jnp.float32), 0.5, 1.5).astype(jnp.bfloat16)
    w_router = noise(key_list[8], (D, E), (2 * D) ** -0.5, 0.15625)
    w_in = noise(key_list[9], (E, D, FF), D ** -0.5, 0.21875, ((2, 2),))
    w_out = noise(key_list[10], (E, FF, D), (max(FF // 192, 1)) ** -0.5, 1.5, ((1, 2),))
    cotangent = heavy_noise(key_list[11], (TOKENS, D), 1.0, 6.0, ((0, 16),), (0, 1, 16, 2.0))
    seq_lengths = draw_seq_lengths(jax.random.fold_in(key_list[14], 71), 0)
    expert_ids = draw_expert_ids(jax.random.fold_in(key_list[14], 71), 0)
    return dict(tokens=tokens, gain_attn=gain_attn, w_query=w_query, w_key=w_key, w_value=w_value, w_output=w_output, position_table=position_table, gain_moe=gain_moe, w_router=w_router, w_in=w_in, w_out=w_out, cotangent=cotangent, seq_lengths=seq_lengths, expert_ids=expert_ids)


EPS = 1e-06
THRESHOLDS = (12, 16, 23, 32, 46, 64, 91)
HIGHEST = lax.Precision.HIGHEST

@jax.custom_vjp
def low(v):
    return lax.optimization_barrier(v.astype(jnp.bfloat16)).astype(jnp.float32)

@jax.custom_vjp
def low_back(v):
    return v

def low_keep(v):
    return (low(v), None)

def low_pass(kept, grad):
    return (grad,)

def back_keep(v):
    return (v, None)

def back_low(kept, grad):
    return (low(grad),)
low.defvjp(low_keep, low_pass)
low_back.defvjp(back_keep, back_low)

def layout(lengths, count):
    ends = jnp.cumsum(lengths)
    places = jnp.arange(count, dtype=jnp.int32)
    after = places[:, None] >= ends[None, :]
    segment = lax.optimization_barrier(jnp.sum(after.astype(jnp.int32), axis=1))
    begin = lax.optimization_barrier(jnp.sum(jnp.where(after, lengths[None, :], 0), axis=1))
    return (segment.astype(jnp.int32), (places - begin).astype(jnp.int32))

def relative_bucket(query_pos, key_pos):
    offset = key_pos[None, :] - query_pos[:, None]
    distance = jnp.abs(offset)
    far_side = 8 + sum(((distance >= edge).astype(jnp.int32) for edge in THRESHOLDS))
    near = jnp.where(distance < 8, distance, far_side)
    return (jnp.where(offset > 0, NB // 2, 0) + near).astype(jnp.int32)

def capacity_slots(expert_ids):
    count = expert_ids.shape[0]
    chosen = (expert_ids[:, None] == jnp.arange(E, dtype=jnp.int32)[None, :]).astype(jnp.int32)
    before = jnp.cumsum(chosen, axis=0) - chosen
    rank = lax.optimization_barrier(jnp.sum(before * chosen, axis=1))
    kept = rank < CAP
    flat = expert_ids * CAP + rank
    target = jnp.where(kept, flat, E * CAP).astype(jnp.int32)
    source = jnp.zeros((E * CAP,), jnp.int32).at[target].set(jnp.arange(count, dtype=jnp.int32), mode='drop')
    filled = jnp.zeros((E * CAP,), jnp.int32).at[target].set(1, mode='drop')
    return (kept, jnp.where(kept, flat, 0).astype(jnp.int32), source, filled, chosen)

def norm_rows(values, gain):
    return values * lax.rsqrt(lax.optimization_barrier(jnp.mean(values * values, axis=-1, keepdims=True)) + EPS) * gain

def matmul(left, right):
    return jnp.dot(left, right, precision=HIGHEST)

def forward(inputs, gain_one, w_query, w_key, w_value, w_output, table, gain_two, w_router, w_in, w_out, segment, position, kept, flat, source, filled, chosen):
    count = inputs.shape[0]
    normed = low(norm_rows(inputs, gain_one))
    query = low(low_back(matmul(normed, w_query))).reshape(count, HEADS, HEAD)
    keys = low(low_back(matmul(normed, w_key))).reshape(count, HEADS, HEAD)
    values = low(low_back(matmul(normed, w_value))).reshape(count, HEADS, HEAD)
    bias = table[relative_bucket(position, position)]
    scores = jnp.einsum('qhd,khd->hqk', query, keys, precision=HIGHEST) + jnp.transpose(bias, (2, 0, 1))
    allowed = segment[:, None] == segment[None, :]
    scores = low_back(jnp.where(allowed[None], scores, -1000000000.0))
    probs = jax.nn.softmax(scores, axis=-1)
    context = jnp.einsum('hqk,khd->qhd', low(probs), values, precision=HIGHEST).reshape(count, HEADS * HEAD)
    context = low(low_back(context))
    middle = inputs + low_back(matmul(context, w_output))
    normed_two = low(norm_rows(middle, gain_two))
    router = jax.nn.softmax(low_back(matmul(normed_two, w_router)), axis=-1)
    gate = lax.optimization_barrier(jnp.sum(router * chosen, axis=1, keepdims=True))
    dispatch = (normed_two[source] * filled[:, None]).reshape(E, CAP, -1)
    pre_act = low_back(jnp.einsum('ecd,edf->ecf', dispatch, w_in, precision=HIGHEST))
    hidden = low(jax.nn.gelu(pre_act))
    expert_out = jnp.einsum('ecf,efd->ecd', hidden, w_out, precision=HIGHEST).reshape(E * CAP, -1)
    expert_full = low_back(expert_out[flat] * kept[:, None])
    return middle + gate * expert_full

def reference(tokens, gain_attn, w_query, w_key, w_value, w_output, position_table, gain_moe, w_router, w_in, w_out, cotangent, seq_lengths, expert_ids):
    params = tuple((item.astype(jnp.float32) for item in (gain_attn, w_query, w_key, w_value, w_output, position_table, gain_moe, w_router, w_in, w_out)))
    rows = tokens.astype(jnp.float32).reshape(N_DP, TOK_DEV, D)
    seeds = cotangent.astype(jnp.float32).reshape(N_DP, TOK_DEV, D)
    routes = expert_ids.reshape(N_DP, TOK_DEV)

    def one_batch(carry, items):
        inputs, grad_seed, lengths, route = items
        segment, position = layout(lengths, TOK_DEV)
        kept, flat, source, filled, chosen = capacity_slots(route)

        def run(values, *weights):
            return forward(values, *weights, segment, position, kept.astype(jnp.float32), flat, source, filled.astype(jnp.float32), chosen.astype(jnp.float32))
        output, pull = jax.vjp(run, inputs, *params)
        grads = pull(grad_seed)
        carry = tuple((total + piece for total, piece in zip(carry, grads[1:])))
        return (carry, (output.astype(jnp.bfloat16), grads[0]))
    initial = tuple((jnp.zeros_like(item) for item in params))
    totals, (mixed, grad_tokens) = lax.scan(one_batch, initial, (rows, seeds, seq_lengths, routes))
    return (mixed.reshape(TOKENS, D), grad_tokens.reshape(TOKENS, D), totals[0], totals[1], totals[2], totals[3], totals[4], totals[5], totals[6], totals[7], totals[8], totals[9])
```

```python
import jax
import jax.numpy as jnp
from jax import lax
from jax.sharding import PartitionSpec as P

HEAD = 64
NB = 32
E = 4
CAP = 160
CORES = 2
PAIR = 2
LOCAL = E // CORES

EPS = 1e-06
THRESHOLDS = (12, 16, 23, 32, 46, 64, 91)
F32 = jnp.float32
BF16 = jnp.bfloat16


def segments(lengths, count):
    places = jnp.arange(count, dtype=jnp.int32)
    entry = jnp.arange(lengths.shape[0], dtype=jnp.int32)
    ends = jnp.sum(jnp.where(entry[None, :] <= entry[:, None], lengths[None, :], 0), axis=1)
    return jnp.sum((places[:, None] >= ends[None, :]).astype(jnp.int32), axis=1)


def relative_bucket(query_pos, key_pos):
    offset = key_pos[None, :] - query_pos[:, None]
    distance = jnp.abs(offset)
    far_side = 8 + sum(((distance >= edge).astype(jnp.int32) for edge in THRESHOLDS))
    near = jnp.where(distance < 8, distance, far_side)
    return jnp.where(offset > 0, NB // 2, 0) + near


def ranks(expert_ids):
    place = jnp.arange(expert_ids.shape[0], dtype=jnp.int32)
    earlier = (expert_ids[:, None] == expert_ids[None, :]) & (place[None, :] < place[:, None])
    return jnp.sum(earlier.astype(jnp.int32), axis=1)


def norm_rows(values, gain):
    return values * lax.rsqrt(jnp.mean(values * values, axis=-1, keepdims=True) + EPS) * gain


def mm(spec, left, right, precision=None):
    return jnp.einsum(spec, left, right, preferred_element_type=F32, precision=precision)


def solution(mesh):
    n_dp, n_mp = mesh.shape["dp"], mesh.shape["mp"]
    line = n_dp // (CORES * PAIR)

    def swap(value, stride):
        return lax.ppermute(value, "dp", [(i, i ^ stride) for i in range(n_dp)])

    def mp_other(value):
        return lax.ppermute(value, "mp", [(0, 1), (1, 0)])

    def mp_sum(value):
        return value + mp_other(value) if n_mp == 2 else lax.psum(value, "mp")

    def dp_sum(value):
        if n_dp & (n_dp - 1):
            return lax.psum(value, "dp")
        stride = 1
        while stride < n_dp:
            value = value + swap(value, stride)
            stride *= 2
        return value

    def shards(
        tokens,
        gain_attn,
        w_query,
        w_key,
        w_value,
        w_output,
        position_table,
        gain_moe,
        w_router,
        w_in,
        w_out,
        cotangent,
        seq_lengths,
        expert_ids,
    ):
        device = lax.axis_index("dp")
        core = device % CORES
        side = (device // CORES) % PAIR
        row = device // (CORES * PAIR)
        count, width = tokens.shape
        share = width // n_dp
        heads = position_table.shape[1]
        inner = heads * HEAD

        def pick(value, index, axis):
            return lax.dynamic_index_in_dim(value, index, axis, keepdims=False)

        def flow(own, up):
            got = None
            for step in range(1, line):
                if up:
                    index = jnp.minimum(line - step + row, line - 1)
                    hops = [(i, i + 1) for i in range(step)]
                else:
                    index = jnp.maximum(step - line + row, 0)
                    hops = [(line - 1 - i, line - 2 - i) for i in range(step)]
                piece = pick(own, index, 0)
                if got is not None:
                    piece = piece + got
                block = CORES * PAIR
                got = lax.ppermute(
                    piece, "dp", [(a * block + k, b * block + k) for a, b in hops for k in range(block)]
                )
            return got

        def line_sum(own):
            if line == 1:
                return own[0]
            if line > 4:
                block = CORES * PAIR
                groups = [[r * block + k for r in range(line)] for k in range(block)]
                return lax.psum_scatter(own, "dp", scatter_dimension=0, axis_index_groups=groups)
            return pick(own, row, 0) + flow(own, True) + flow(own, False)

        def chip_sum(own):
            got = swap(pick(own, 1 - side, 1), CORES)
            return line_sum(pick(own, side, 1) + got)

        def expert_sum(grad):
            own = chip_sum(grad.reshape(line, PAIR, CORES * share, -1)).reshape(CORES, share, -1)
            return pick(own, core, 0), swap(pick(own, 1 - core, 0), 1)

        def dense_sum(grad):
            own = grad.reshape(line, PAIR, CORES, share, -1)
            got = swap(pick(own, 1 - core, 2), 1)
            return chip_sum(pick(own, core, 2) + got)

        segment = segments(seq_lengths[0], count)
        place = jnp.arange(count, dtype=jnp.int32)
        inputs = tokens.astype(F32)
        gain_one = gain_attn.astype(F32)
        gain_two = gain_moe.astype(F32)
        bucket_ids = jnp.arange(NB, dtype=jnp.int32)
        normed = norm_rows(inputs, gain_one).astype(BF16)
        query = mm("td,dc->tc", normed, w_query).astype(BF16).reshape(count, heads, HEAD)
        keys = mm("td,dc->tc", normed, w_key).astype(BF16).reshape(count, heads, HEAD)
        values = mm("td,dc->tc", normed, w_value).astype(BF16).reshape(count, heads, HEAD)

        bucket = relative_bucket(place, place)
        onehot = (bucket[:, :, None] == bucket_ids[None, None, :]).astype(BF16)
        allowed = segment[:, None] == segment[None, :]

        def all_scores():
            bias = mm("qkb,bh->hqk", onehot, position_table)
            scores = mm("qhd,khd->hqk", query, keys) + bias
            return jnp.where(allowed[None], scores, -1000000000.0)

        scores = all_scores()
        peak = jnp.max(scores, axis=-1, keepdims=True)
        total = peak + jnp.log(jnp.sum(jnp.exp(scores - peak), axis=-1, keepdims=True))
        probs = jnp.exp(scores - total).astype(BF16)
        context = mm("hqk,khd->qhd", probs, values).reshape(count, inner).astype(BF16)
        middle = inputs + mp_sum(mm("tc,cd->td", context, w_output))

        rank = ranks(expert_ids)
        local = (expert_ids - LOCAL * core) % E
        slot = jnp.where(rank < CAP, local * CAP + rank, -1)
        select = jnp.arange(E * CAP, dtype=jnp.int32)[:, None] == slot[None, :]
        select_low = select.astype(BF16)
        select_full = select.astype(F32)
        picked = (expert_ids[:, None] == jnp.arange(E, dtype=jnp.int32)[None, :]).astype(F32)
        my_in = lax.dynamic_slice_in_dim(w_in, LOCAL * core, LOCAL, 0)
        my_out = lax.dynamic_slice_in_dim(w_out, LOCAL * core, LOCAL, 0)

        half = LOCAL * CAP

        def to_experts(rows):
            slots = mm("st,td->sd", select_low, rows)
            return slots[:half], swap(slots[half:], 1)

        def scaled(parts, weight):
            both = [
                (part * scale[:, None]).reshape(LOCAL, CAP, width)
                for part, scale in zip(parts, weight)
            ]
            return jnp.concatenate(both, axis=1).astype(BF16)

        def slot_values(values):
            slots = jnp.sum(jnp.where(select, values[None, :], 0.0), axis=1)
            return slots[:half], swap(slots[half:], 1)

        live = slot_values(jnp.ones((count,), F32))
        seed_slots = to_experts(cotangent)

        def to_tokens(slots):
            got = swap(slots[:, CAP:], 1)
            both = jnp.concatenate([slots[:, :CAP], got], axis=0).reshape(E * CAP, width)
            return mm("st,sd->td", select_full, both, lax.Precision.HIGH)

        normed_two = norm_rows(middle, gain_two).astype(BF16)
        dispatch = scaled(to_experts(normed_two), live)
        logits = mm("td,de->te", normed_two, w_router)
        router = jax.nn.softmax(logits, axis=-1)
        gate = jnp.sum(router * picked, axis=1, keepdims=True)
        grad_seed = cotangent.astype(F32)
        slot_grad = scaled(seed_slots, slot_values(gate[:, 0]))

        pre_act = mm("ecd,edf->ecf", dispatch, my_in)
        hidden, gelu_pull = jax.vjp(jax.nn.gelu, pre_act)
        hidden = hidden.astype(BF16)
        grad_out_rows = mm("ecd,ecf->edf", slot_grad, hidden)
        out_sums = [expert_sum(grad_out_rows[k]) for k in range(LOCAL)]
        hidden_grad = mm("ecd,efd->ecf", slot_grad, my_out)
        pre_grad = gelu_pull(hidden_grad)[0].astype(BF16)
        grad_in_rows = mm("ecd,ecf->edf", dispatch, pre_grad)
        in_sums = [expert_sum(grad_in_rows[k]) for k in range(LOCAL)]
        expert_part = to_tokens(mm("ecf,efd->ecd", hidden, my_out))
        back_part = to_tokens(mm("ecf,edf->ecd", pre_grad, my_in))
        gate_grad = mp_sum(jnp.sum(grad_seed * expert_part, axis=1, keepdims=True))
        expert_back = mp_sum(back_part)
        mixed = (middle + gate * mp_sum(expert_part)).astype(BF16)

        logit_grad = (gate_grad * gate * (picked - router)).astype(BF16)
        grad_router = mm("td,te->de", normed_two, logit_grad)
        second_grad = expert_back + mm("te,de->td", logit_grad, w_router)
        _, second_pull = jax.vjp(norm_rows, middle, gain_two)
        middle_grad, grad_gain_two = second_pull(second_grad)
        middle_grad = middle_grad + grad_seed
        attn_grad = middle_grad.astype(BF16)
        grad_output_rows = mm("td,tc->dc", attn_grad, context)
        context_grad = (
            mm("td,cd->tc", attn_grad, w_output).astype(BF16).reshape(count, heads, HEAD)
        )
        probs = jnp.exp(all_scores() - total)
        prob_grad = mm("qhd,khd->hqk", context_grad, values)
        centre = jnp.sum(probs * prob_grad, axis=-1, keepdims=True)
        score_grad = (probs * (prob_grad - centre)).astype(BF16)
        query_grad = mm("hqk,khd->qhd", score_grad, keys).reshape(count, inner).astype(BF16)
        key_grad = mm("hqk,qhd->khd", score_grad, query).reshape(count, inner).astype(BF16)
        value_grad = (
            mm("hqk,qhd->khd", probs.astype(BF16), context_grad).reshape(count, inner).astype(BF16)
        )
        grad_table = mm("hqk,qkb->bh", score_grad, onehot)
        first_part = (
            mm("tc,dc->td", query_grad, w_query)
            + mm("tc,dc->td", key_grad, w_key)
            + mm("tc,dc->td", value_grad, w_value)
        )
        first_grad = mp_sum(first_part)
        grad_query_rows = mm("td,tc->dc", normed, query_grad)
        grad_key_rows = mm("td,tc->dc", normed, key_grad)
        grad_value_rows = mm("td,tc->dc", normed, value_grad)
        dense = dense_sum(
            jnp.concatenate(
                [grad_query_rows, grad_key_rows, grad_value_rows, grad_output_rows], axis=1
            )
        )
        _, first_pull = jax.vjp(norm_rows, inputs, gain_one)
        input_grad, _ = first_pull(first_grad)
        grad_tokens = middle_grad + input_grad
        grad_gain_one = mp_sum(first_pull(first_part)[1])
        small = jnp.concatenate(
            [
                grad_gain_one[None],
                grad_gain_two[None],
                grad_router.T,
                jnp.pad(grad_table.T, ((0, 0), (0, width - NB))),
            ],
            axis=0,
        )
        small = dp_sum(small)
        table_total = small[2 + E :, :NB].T
        small = lax.dynamic_slice_in_dim(small[: 2 + E], device * share, share, 1)

        def by_expert(sums):
            mine = jnp.stack([own for own, _ in sums])
            other = jnp.stack([got for _, got in sums])
            first = core == 0
            return jnp.concatenate(
                [jnp.where(first, mine, other), jnp.where(first, other, mine)], axis=0
            )

        return (
            mixed,
            grad_tokens,
            small[0],
            dense[:, :inner],
            dense[:, inner : 2 * inner],
            dense[:, 2 * inner : 3 * inner],
            dense[:, 3 * inner :].T,
            table_total,
            small[1],
            small[2:].T,
            by_expert(in_sums),
            jnp.swapaxes(by_expert(out_sums), 1, 2),
        )

    return jax.shard_map(
        shards,
        mesh=mesh,
        in_specs=(
            P("dp", None),
            P(),
            P(None, "mp"),
            P(None, "mp"),
            P(None, "mp"),
            P("mp", None),
            P(None, "mp"),
            P(),
            P(),
            P(None, None, "mp"),
            P(None, "mp", None),
            P("dp", None),
            P("dp", None),
            P("dp"),
        ),
        out_specs=(
            P("dp", None),
            P("dp", None),
            P("dp"),
            P("dp", "mp"),
            P("dp", "mp"),
            P("dp", "mp"),
            P("mp", "dp"),
            P(None, "mp"),
            P("dp"),
            P("dp", None),
            P(None, "dp", "mp"),
            P(None, "mp", "dp"),
        ),
        check_vma=False,
    )
```

```python
import jax
import jax.numpy as jnp
from jax import lax
from jax.sharding import PartitionSpec as P

HEAD = 64
NB = 32
E = 4
CAP = 160
CORES = 2
PAIR = 2
LOCAL = E // CORES

EPS = 1e-06
THRESHOLDS = (12, 16, 23, 32, 46, 64, 91)
F32 = jnp.float32
BF16 = jnp.bfloat16


def segments(lengths, count):
    places = jnp.arange(count, dtype=jnp.int32)
    entry = jnp.arange(lengths.shape[0], dtype=jnp.int32)
    ends = jnp.sum(jnp.where(entry[None, :] <= entry[:, None], lengths[None, :], 0), axis=1)
    return jnp.sum((places[:, None] >= ends[None, :]).astype(jnp.int32), axis=1)


def relative_bucket(query_pos, key_pos):
    offset = key_pos[None, :] - query_pos[:, None]
    distance = jnp.abs(offset)
    far_side = 8 + sum(((distance >= edge).astype(jnp.int32) for edge in THRESHOLDS))
    near = jnp.where(distance < 8, distance, far_side)
    return jnp.where(offset > 0, NB // 2, 0) + near


def ranks(expert_ids):
    place = jnp.arange(expert_ids.shape[0], dtype=jnp.int32)
    earlier = (expert_ids[:, None] == expert_ids[None, :]) & (place[None, :] < place[:, None])
    return jnp.sum(earlier.astype(jnp.int32), axis=1)


def norm_rows(values, gain):
    return values * lax.rsqrt(jnp.mean(values * values, axis=-1, keepdims=True) + EPS) * gain


def mm(spec, left, right, precision=None):
    return jnp.einsum(spec, left, right, preferred_element_type=F32, precision=precision)


def solution(mesh):
    n_dp, n_mp = mesh.shape["dp"], mesh.shape["mp"]
    line = n_dp // (CORES * PAIR)

    def swap(value, stride):
        return lax.ppermute(value, "dp", [(i, i ^ stride) for i in range(n_dp)])

    def mp_other(value):
        return lax.ppermute(value, "mp", [(0, 1), (1, 0)])

    def mp_sum(value):
        return value + mp_other(value) if n_mp == 2 else lax.psum(value, "mp")

    def dp_sum(value):
        if n_dp & (n_dp - 1):
            return lax.psum(value, "dp")
        stride = 1
        while stride < n_dp:
            value = value + swap(value, stride)
            stride *= 2
        return value

    def shards(
        tokens,
        gain_attn,
        w_query,
        w_key,
        w_value,
        w_output,
        position_table,
        gain_moe,
        w_router,
        w_in,
        w_out,
        cotangent,
        seq_lengths,
        expert_ids,
    ):
        device = lax.axis_index("dp")
        core = device % CORES
        side = (device // CORES) % PAIR
        row = device // (CORES * PAIR)
        count, width = tokens.shape
        share = width // n_dp
        heads = position_table.shape[1]
        inner = heads * HEAD

        def pick(value, index, axis):
            return lax.dynamic_index_in_dim(value, index, axis, keepdims=False)

        def cut(value, index, size):
            return lax.dynamic_slice_in_dim(value, index, size, 1)

        low = row < line // 2

        def hop(value, pairs):
            block = CORES * PAIR
            return lax.ppermute(
                value, "dp", [(a * block + k, b * block + k) for a, b in pairs for k in range(block)]
            )

        def line_in(own):
            if line == 4:
                piece = cut(own, jnp.where(low, 1, 0), 3)
                return own, (hop(piece, [(0, 1), (3, 2)]),)
            block = CORES * PAIR
            groups = [[r * block + k for r in range(line)] for k in range(block)]
            total = lax.psum_scatter(own, "dp", scatter_dimension=1, axis_index_groups=groups)
            return own, (total,)

        def line_middle(state, *deps):
            own, got = state
            if line == 4:
                piece = cut(own, jnp.where(low, 2, 0), 2) + cut(got[0], jnp.where(low, 1, 0), 2)
                got = (*got, hop(after(piece, *deps), [(1, 2), (2, 1)]))
            return own, got

        def line_out(state, *deps):
            own, got = state
            if line == 4:
                piece = cut(own, jnp.where(low, 0, 3), 1) + cut(got[1], jnp.where(low, 0, 1), 1)
                got = (*got, hop(after(piece, *deps), [(1, 0), (2, 3)]))
            return own, got

        def line_end(state):
            own, got = state
            if line != 4:
                return got[0]
            return (
                pick(own, row, 1)
                + pick(got[0], jnp.where(low, 0, 2), 1)
                + pick(got[1], jnp.where(low, 1, 0), 1)
                + got[2][:, 0]
            )

        def after(value, *deps):
            return lax.optimization_barrier((value, *deps))[0] if deps else value

        def core_swap(rows):
            rows = rows.reshape(rows.shape[0], CORES, share, -1)
            return pick(rows, core, 1), swap(pick(rows, 1 - core, 1), 1)

        feature = jnp.arange(width, dtype=jnp.int32)
        half_width = width // 2

        def chosen_columns(source):
            return (feature[:, None] == source[None, :]).astype(BF16)

        rest = feature % half_width
        part_side = jnp.where(feature < half_width, 1 - side, side)
        pair_order = chosen_columns(
            (rest // (CORES * share)) * (PAIR * CORES * share)
            + part_side * (CORES * share)
            + rest % (CORES * share)
        )
        part_core = jnp.where(feature < half_width, 1 - core, core)
        part_side = jnp.where(rest < half_width // 2, 1 - side, side)
        rest = rest % (half_width // 2)
        core_order = chosen_columns(
            (rest // share) * (PAIR * CORES * share)
            + part_side * (CORES * share)
            + part_core * share
            + rest % share
        )

        segment = segments(seq_lengths[0], count)
        place = jnp.arange(count, dtype=jnp.int32)
        inputs = tokens.astype(F32)
        gain_one = gain_attn.astype(F32)
        gain_two = gain_moe.astype(F32)
        bucket_ids = jnp.arange(NB, dtype=jnp.int32)
        normed = norm_rows(inputs, gain_one).astype(BF16)
        query = mm("td,dc->tc", normed, w_query).astype(BF16).reshape(count, heads, HEAD)
        keys = mm("td,dc->tc", normed, w_key).astype(BF16).reshape(count, heads, HEAD)
        values = mm("td,dc->tc", normed, w_value).astype(BF16).reshape(count, heads, HEAD)

        bucket = relative_bucket(place, place)
        onehot = (bucket[:, :, None] == bucket_ids[None, None, :]).astype(BF16)
        allowed = segment[:, None] == segment[None, :]

        def all_scores():
            bias = mm("qkb,bh->hqk", onehot, position_table)
            scores = mm("qhd,khd->hqk", query, keys) + bias
            return jnp.where(allowed[None], scores, -1000000000.0)

        scores = all_scores()
        peak = jnp.max(scores, axis=-1, keepdims=True)
        total = peak + jnp.log(jnp.sum(jnp.exp(scores - peak), axis=-1, keepdims=True))
        probs = jnp.exp(scores - total).astype(BF16)
        context = mm("hqk,khd->qhd", probs, values).reshape(count, inner).astype(BF16)
        middle = inputs + mp_sum(mm("tc,cd->td", context, w_output))

        rank = ranks(expert_ids)
        local = (expert_ids - LOCAL * core) % E
        slot = jnp.where(rank < CAP, local * CAP + rank, -1)
        select = jnp.arange(E * CAP, dtype=jnp.int32)[:, None] == slot[None, :]
        select_low = select.astype(BF16)
        select_full = select.astype(F32)
        picked = (expert_ids[:, None] == jnp.arange(E, dtype=jnp.int32)[None, :]).astype(F32)
        my_in = lax.dynamic_slice_in_dim(w_in, LOCAL * core, LOCAL, 0)
        my_out = lax.dynamic_slice_in_dim(w_out, LOCAL * core, LOCAL, 0)

        half = LOCAL * CAP

        def to_experts(rows):
            slots = mm("st,td->sd", select_low, rows)
            return slots[:half], swap(slots[half:], 1)

        def scaled(parts, weight):
            both = [
                (part * scale[:, None]).reshape(LOCAL, CAP, width)
                for part, scale in zip(parts, weight)
            ]
            return jnp.concatenate(both, axis=1).astype(BF16)

        def slot_values(values):
            slots = jnp.sum(jnp.where(select, values[None, :], 0.0), axis=1)
            return slots[:half], swap(slots[half:], 1)

        live = slot_values(jnp.ones((count,), F32))
        seed_slots = to_experts(cotangent)

        def to_tokens(slots):
            got = swap(slots[:, CAP:], 1)
            both = jnp.concatenate([slots[:, :CAP], got], axis=0).reshape(E * CAP, width)
            return mm("st,sd->td", select_full, both, lax.Precision.HIGH)

        normed_two = norm_rows(middle, gain_two).astype(BF16)
        dispatch = scaled(to_experts(normed_two), live)
        logits = mm("td,de->te", normed_two, w_router)
        router = jax.nn.softmax(logits, axis=-1)
        gate = jnp.sum(router * picked, axis=1, keepdims=True)
        grad_seed = cotangent.astype(F32)
        slot_grad = scaled(seed_slots, slot_values(gate[:, 0]))

        pre_act = mm("ecd,edf->ecf", dispatch, my_in)
        hidden, gelu_pull = jax.vjp(jax.nn.gelu, pre_act)
        hidden = hidden.astype(BF16)
        units = hidden.shape[2]
        slot_grad_pair = mm("ecd,dk->eck", slot_grad, pair_order).astype(BF16)

        def grads(left, right):
            return mm("ecd,ecf->edf", left, right)

        def paired(left, right, got):
            total = grads(left[:, :, half_width:], right) + got
            return total.reshape(total.shape[0], line, CORES * share, -1)

        out_first = slot_grad_pair[:1], hidden[:1]
        out_second = slot_grad_pair[1:], hidden[1:]
        sent_out_first = grads(out_first[0][:, :, :half_width], out_first[1])
        got_out_first = swap(sent_out_first, CORES)

        hidden_grad = mm("ecd,efd->ecf", after(slot_grad, sent_out_first), my_out)
        pre_grad = gelu_pull(hidden_grad)[0].astype(BF16)
        back_slots = mm("ecf,edf->ecd", pre_grad, my_in)
        part_slots = mm("ecf,efd->ecd", hidden, my_out)
        back_part = to_tokens(back_slots)
        expert_part = to_tokens(part_slots)
        cut_at = units * 2 // 3
        own = grads(dispatch, after(pre_grad, back_slots)[:, :, cut_at:])
        state_z = line_in(own.reshape(LOCAL, line, PAIR * CORES * share, -1))
        gate_grad = mp_sum(jnp.sum(grad_seed * expert_part, axis=1, keepdims=True))
        expert_back = mp_sum(back_part)
        dispatch_pair = mm("ecd,dk->eck", dispatch, pair_order).astype(BF16)
        in_first = dispatch_pair, pre_grad[:, :, : cut_at // 2]
        in_second = dispatch_pair, pre_grad[:, :, cut_at // 2 : cut_at]

        sent_out_second = after(
            grads(out_second[0][:, :, :half_width], out_second[1]), got_out_first, back_part
        )
        got_out_second = swap(sent_out_second, CORES)
        state_a = line_in(after(paired(*out_first, got_out_first), sent_out_second))

        logit_grad = (gate_grad * gate * (picked - router)).astype(BF16)
        grad_router = mm("td,te->de", normed_two, logit_grad)
        second_grad = expert_back + mm("te,de->td", logit_grad, w_router)
        _, second_pull = jax.vjp(norm_rows, middle, gain_two)
        middle_grad, grad_gain_two = second_pull(second_grad)
        middle_grad = middle_grad + grad_seed
        attn_grad = middle_grad.astype(BF16)
        context_grad = (
            mm("td,cd->tc", attn_grad, w_output).astype(BF16).reshape(count, heads, HEAD)
        )
        probs = jnp.exp(all_scores() - total)
        prob_grad = mm("qhd,khd->hqk", context_grad, values)
        centre = jnp.sum(probs * prob_grad, axis=-1, keepdims=True)
        score_grad = (probs * (prob_grad - centre)).astype(BF16)
        query_grad = mm("hqk,khd->qhd", score_grad, keys).reshape(count, inner).astype(BF16)
        key_grad = mm("hqk,qhd->khd", score_grad, query).reshape(count, inner).astype(BF16)
        value_grad = (
            mm("hqk,qhd->khd", probs.astype(BF16), context_grad).reshape(count, inner).astype(BF16)
        )
        grad_table = mm("hqk,qkb->bh", score_grad, onehot)
        first_part = (
            mm("tc,dc->td", query_grad, w_query)
            + mm("tc,dc->td", key_grad, w_key)
            + mm("tc,dc->td", value_grad, w_value)
        )
        first_grad = mp_sum(first_part)
        qkv_grad = jnp.concatenate([query_grad, key_grad, value_grad], axis=1)
        normed_core = mm("td,dk->tk", normed, core_order).astype(BF16)
        attn_grad_core = mm("td,dk->tk", attn_grad, core_order).astype(BF16)

        def dense(columns):
            return jnp.concatenate(
                [
                    mm("td,tc->dc", normed_core[:, columns], qkv_grad),
                    mm("td,tc->dc", attn_grad_core[:, columns], context),
                ],
                axis=1,
            )

        sent_dense = after(dense(slice(0, half_width)), first_part)
        got_dense = swap(sent_dense, 1)

        state_z = line_middle(state_z, sent_dense)
        sent_in_first = after(
            grads(in_first[0][:, :, :half_width], in_first[1]), got_out_second, sent_dense
        )
        got_in_first = swap(sent_in_first, CORES)
        state_b = line_in(after(paired(*out_second, got_out_second), sent_in_first))
        dense_half = dense(slice(half_width, width)) + got_dense
        state_a = line_middle(state_a, sent_in_first)
        mixed_part = after(expert_part, first_grad)
        mixed = (middle + gate * mp_sum(mixed_part)).astype(BF16)
        state_z = line_out(state_z, sent_in_first)
        state_a = line_out(state_a, state_z[1][-1])
        state_b = line_middle(state_b, state_z[1][-1])
        sent_in_second = after(
            grads(in_second[0][:, :, :half_width], in_second[1]), got_in_first, state_z[1][-1]
        )
        got_in_second = swap(sent_in_second, CORES)
        state_c = line_in(after(paired(*in_first, got_in_first), sent_in_second))
        sums_a = core_swap(line_end(state_a))
        state_b = line_out(state_b, sent_in_second)
        sent_late = after(dense_half[: half_width // 2], got_in_second)
        got_late = swap(sent_late, CORES)
        state_d = line_in(after(paired(*in_second, got_in_second), sent_late))
        state_c = line_middle(state_c, sent_late)
        sums_b = core_swap(line_end(state_b))
        rows_z = line_end(state_z).reshape(LOCAL, PAIR, CORES * share, -1)
        got_z = swap(after(pick(rows_z, 1 - side, 1), got_late), CORES)
        state_e = line_in(
            (dense_half[half_width // 2 :] + got_late).reshape(1, line, share, -1)
        )
        state_c = line_out(state_c, got_late)
        state_d = line_middle(state_d, got_late)
        sums_z = core_swap(pick(rows_z, side, 1) + got_z)
        sums_c = core_swap(line_end(state_c))
        state_e = line_middle(state_e)
        state_d = line_out(state_d)
        state_e = line_out(state_e)
        sums_d = core_swap(line_end(state_d))
        dense_sum = line_end(state_e)[0]
        out_sums = [jnp.concatenate(pair, axis=0) for pair in zip(sums_a, sums_b)]
        in_sums = [jnp.concatenate(three, axis=2) for three in zip(sums_c, sums_d, sums_z)]

        _, first_pull = jax.vjp(norm_rows, inputs, gain_one)
        input_grad, _ = first_pull(first_grad)
        grad_tokens = middle_grad + input_grad
        grad_gain_one = mp_sum(first_pull(first_part)[1])
        small = jnp.concatenate(
            [
                grad_gain_one[None],
                grad_gain_two[None],
                grad_router.T,
                jnp.pad(grad_table.T, ((0, 0), (0, width - NB))),
            ],
            axis=0,
        )
        small = dp_sum(small)
        table_total = small[2 + E :, :NB].T
        small = lax.dynamic_slice_in_dim(small[: 2 + E], device * share, share, 1)

        def by_expert(sums):
            mine, other = sums
            first = core == 0
            return jnp.concatenate(
                [jnp.where(first, mine, other), jnp.where(first, other, mine)], axis=0
            )

        return (
            mixed,
            grad_tokens,
            small[0],
            dense_sum[:, :inner],
            dense_sum[:, inner : 2 * inner],
            dense_sum[:, 2 * inner : 3 * inner],
            dense_sum[:, 3 * inner :].T,
            table_total,
            small[1],
            small[2:].T,
            by_expert(in_sums),
            jnp.swapaxes(by_expert(out_sums), 1, 2),
        )

    return jax.shard_map(
        shards,
        mesh=mesh,
        in_specs=(
            P("dp", None),
            P(),
            P(None, "mp"),
            P(None, "mp"),
            P(None, "mp"),
            P("mp", None),
            P(None, "mp"),
            P(),
            P(),
            P(None, None, "mp"),
            P(None, "mp", None),
            P("dp", None),
            P("dp", None),
            P("dp"),
        ),
        out_specs=(
            P("dp", None),
            P("dp", None),
            P("dp"),
            P("dp", "mp"),
            P("dp", "mp"),
            P("dp", "mp"),
            P("mp", "dp"),
            P(None, "mp"),
            P("dp"),
            P("dp", None),
            P(None, "dp", "mp"),
            P(None, "mp", "dp"),
        ),
        check_vma=False,
    )
```

```python
import jax
import jax.numpy as jnp
from jax import lax
from jax.sharding import PartitionSpec as P

HEAD = 64
NB = 32
E = 4
CAP = 160
CORES = 2
PAIR = 2
LINE = 2
LOCAL = E // CORES

EPS = 1e-06
THRESHOLDS = (12, 16, 23, 32, 46, 64, 91)
F32 = jnp.float32
BF16 = jnp.bfloat16


def segments(lengths, count):
    places = jnp.arange(count, dtype=jnp.int32)
    entry = jnp.arange(lengths.shape[0], dtype=jnp.int32)
    ends = jnp.sum(jnp.where(entry[None, :] <= entry[:, None], lengths[None, :], 0), axis=1)
    return jnp.sum((places[:, None] >= ends[None, :]).astype(jnp.int32), axis=1)


def relative_bucket(query_pos, key_pos):
    offset = key_pos[None, :] - query_pos[:, None]
    distance = jnp.abs(offset)
    far_side = 8 + sum(((distance >= edge).astype(jnp.int32) for edge in THRESHOLDS))
    near = jnp.where(distance < 8, distance, far_side)
    return jnp.where(offset > 0, NB // 2, 0) + near


def ranks(expert_ids):
    place = jnp.arange(expert_ids.shape[0], dtype=jnp.int32)
    earlier = (expert_ids[:, None] == expert_ids[None, :]) & (place[None, :] < place[:, None])
    return jnp.sum(earlier.astype(jnp.int32), axis=1)


def norm_rows(values, gain):
    return values * lax.rsqrt(jnp.mean(values * values, axis=-1, keepdims=True) + EPS) * gain


def mm(spec, left, right, precision=None):
    return jnp.einsum(spec, left, right, preferred_element_type=F32, precision=precision)


def solution(mesh):
    n_dp, n_mp = mesh.shape["dp"], mesh.shape["mp"]
    bits = n_dp.bit_length() - 1

    def swap(value, stride):
        return lax.ppermute(value, "dp", [(i, i ^ stride) for i in range(n_dp)])

    def mp_other(value):
        return lax.ppermute(value, "mp", [(0, 1), (1, 0)])

    def mp_sum(value):
        return value + mp_other(value) if n_mp == 2 else lax.psum(value, "mp")

    def shards(
        tokens,
        gain_attn,
        w_query,
        w_key,
        w_value,
        w_output,
        position_table,
        gain_moe,
        w_router,
        w_in,
        w_out,
        cotangent,
        seq_lengths,
        expert_ids,
    ):
        device = lax.axis_index("dp")
        core = device % CORES
        count, width = tokens.shape
        share = width // n_dp
        heads = position_table.shape[1]
        inner = heads * HEAD

        last = []

        def after(value, *deps):
            return lax.optimization_barrier((value, *deps))[0] if deps else value

        def ready(value):
            value = after(value, *last)
            last[:] = [value]
            return value

        def take(got):
            got = after(got, *last)
            last[:] = [got]
            return got

        def begin(rows, bit):
            half = rows.shape[1] // 2
            return rows[:, half:], swap(ready(rows[:, :half]), 1 << bit)

        def finish(state):
            kept, got = state
            return kept + take(got)

        def line_next(state):
            for bit in range(LINE + 1, bits - 1):
                state = begin(finish(state), bit)
            return begin(finish(state), bits - 1)

        def core_begin(state):
            return begin(finish(state), 0)

        feature = jnp.arange(width, dtype=jnp.int32)
        half_width = width // 2

        def column_order(names):
            source = feature % share
            for place, name in enumerate(names):
                same = (feature // share) >> (bits - 1 - place) & 1
                bit = (device >> name & 1) ^ (1 - same)
                source = source + (bit << name) * share
            return (feature[:, None] == source[None, :]).astype(BF16)

        line_bits = list(range(LINE, bits))
        pair_order = column_order([1, *line_bits, 0])
        line_order = column_order([*line_bits, 1, 0])
        core_order = column_order([0, 1, *line_bits])

        segment = segments(seq_lengths[0], count)
        place = jnp.arange(count, dtype=jnp.int32)
        inputs = tokens.astype(F32)
        gain_one = gain_attn.astype(F32)
        gain_two = gain_moe.astype(F32)
        bucket_ids = jnp.arange(NB, dtype=jnp.int32)
        normed = norm_rows(inputs, gain_one).astype(BF16)
        query = mm("td,dc->tc", normed, w_query).astype(BF16).reshape(count, heads, HEAD)
        keys = mm("td,dc->tc", normed, w_key).astype(BF16).reshape(count, heads, HEAD)
        values = mm("td,dc->tc", normed, w_value).astype(BF16).reshape(count, heads, HEAD)

        bucket = relative_bucket(place, place)
        onehot = (bucket[:, :, None] == bucket_ids[None, None, :]).astype(BF16)
        allowed = segment[:, None] == segment[None, :]

        def all_scores():
            bias = mm("qkb,bh->hqk", onehot, position_table)
            scores = mm("qhd,khd->hqk", query, keys) + bias
            return jnp.where(allowed[None], scores, -1000000000.0)

        scores = all_scores()
        peak = jnp.max(scores, axis=-1, keepdims=True)
        total = peak + jnp.log(jnp.sum(jnp.exp(scores - peak), axis=-1, keepdims=True))
        probs = jnp.exp(scores - total).astype(BF16)
        context = mm("hqk,khd->qhd", probs, values).reshape(count, inner).astype(BF16)
        middle = inputs + mp_sum(mm("tc,cd->td", context, w_output))

        rank = ranks(expert_ids)
        local = (expert_ids - LOCAL * core) % E
        slot = jnp.where(rank < CAP, local * CAP + rank, -1)
        select = jnp.arange(E * CAP, dtype=jnp.int32)[:, None] == slot[None, :]
        select_low = select.astype(BF16)
        select_full = select.astype(F32)
        picked = (expert_ids[:, None] == jnp.arange(E, dtype=jnp.int32)[None, :]).astype(F32)
        my_in = lax.dynamic_slice_in_dim(w_in, LOCAL * core, LOCAL, 0)
        my_out = lax.dynamic_slice_in_dim(w_out, LOCAL * core, LOCAL, 0)

        half = LOCAL * CAP

        def to_experts(rows):
            slots = mm("st,td->sd", select_low, rows)
            return slots[:half], swap(slots[half:], 1)

        def scaled(parts, weight):
            both = [
                (part * scale[:, None]).reshape(LOCAL, CAP, width)
                for part, scale in zip(parts, weight)
            ]
            return jnp.concatenate(both, axis=1).astype(BF16)

        def slot_values(values):
            slots = jnp.sum(jnp.where(select, values[None, :], 0.0), axis=1)
            return slots[:half], swap(slots[half:], 1)

        live = slot_values(jnp.ones((count,), F32))
        seed_slots = to_experts(cotangent)

        def to_tokens(slots):
            got = swap(slots[:, CAP:], 1)
            both = jnp.concatenate([slots[:, :CAP], got], axis=0).reshape(E * CAP, width)
            return mm("st,sd->td", select_full, both, lax.Precision.HIGH)

        normed_two = norm_rows(middle, gain_two).astype(BF16)
        dispatch = scaled(to_experts(normed_two), live)
        logits = mm("td,de->te", normed_two, w_router)
        router = jax.nn.softmax(logits, axis=-1)
        gate = jnp.sum(router * picked, axis=1, keepdims=True)
        grad_seed = cotangent.astype(F32)
        slot_grad = scaled(seed_slots, slot_values(gate[:, 0]))

        pre_act = mm("ecd,edf->ecf", dispatch, my_in)
        hidden, gelu_pull = jax.vjp(jax.nn.gelu, pre_act)
        hidden = hidden.astype(BF16)
        units = hidden.shape[2]
        slot_grad_pair = mm("ecd,dk->eck", slot_grad, pair_order).astype(BF16)

        def grads(left, right):
            return mm("ecd,ecf->edf", left, right)

        def paired(pair, got):
            return grads(pair[0][:, :, mine], pair[1]) + take(got)

        out_first = slot_grad_pair[:1], hidden[:1]
        out_second = slot_grad_pair[1:], hidden[1:]
        other, mine = slice(0, half_width), slice(half_width, width)

        def sent_part(pair):
            return grads(pair[0][:, :, other], pair[1])

        got_a = swap(ready(sent_part(out_first)), PAIR)
        hidden_grad = mm("ecd,efd->ecf", after(slot_grad, *last), my_out)
        pre_grad = gelu_pull(hidden_grad)[0].astype(BF16)
        back_slots = mm("ecf,edf->ecd", pre_grad, my_in)
        part_slots = mm("ecf,efd->ecd", after(hidden, *last), my_out)
        cut_at = units * 2 // 3
        dispatch_pair = mm("ecd,dk->eck", dispatch, pair_order).astype(BF16)
        dispatch_line = mm("ecd,dk->eck", dispatch, line_order).astype(BF16)
        in_first = dispatch_pair, pre_grad[:, :, : cut_at // 2]
        in_second = dispatch_pair, pre_grad[:, :, cut_at // 2 : cut_at]
        in_third = dispatch_line, pre_grad[:, :, cut_at:]
        expert_part = to_tokens(part_slots)
        back_part = to_tokens(back_slots)
        state_z = None, swap(ready(sent_part(in_third)), 1 << LINE)
        gate_part = jnp.sum(grad_seed * expert_part, axis=1)
        gate_rows = jnp.pad(gate_part.reshape(-1, count // 4), ((0, 4), (0, width - count // 4)))
        back = ready(jnp.concatenate([back_part, gate_rows], axis=0))
        back_got = mp_other(back)
        got_b = swap(ready(sent_part(out_second)), PAIR)
        state_z = line_next((grads(in_third[0][:, :, mine], in_third[1]), state_z[1]))
        state_a = begin(paired(out_first, got_a), LINE)
        back_sum = back + take(back_got)
        expert_back = back_sum[:count]
        gate_grad = back_sum[count : count + 4, : count // 4].reshape(count, 1)

        logit_grad = (gate_grad * gate * (picked - router)).astype(BF16)
        grad_router = mm("td,te->de", normed_two, logit_grad)
        second_grad = expert_back + mm("te,de->td", logit_grad, w_router)
        _, second_pull = jax.vjp(norm_rows, middle, gain_two)
        middle_grad, grad_gain_two = second_pull(second_grad)
        middle_grad = middle_grad + grad_seed
        attn_grad = middle_grad.astype(BF16)
        context_grad = (
            mm("td,cd->tc", attn_grad, w_output).astype(BF16).reshape(count, heads, HEAD)
        )
        probs = jnp.exp(all_scores() - total)
        prob_grad = mm("qhd,khd->hqk", context_grad, values)
        centre = jnp.sum(probs * prob_grad, axis=-1, keepdims=True)
        score_grad = (probs * (prob_grad - centre)).astype(BF16)
        query_grad = mm("hqk,khd->qhd", score_grad, keys).reshape(count, inner).astype(BF16)
        key_grad = mm("hqk,qhd->khd", score_grad, query).reshape(count, inner).astype(BF16)
        value_grad = (
            mm("hqk,qhd->khd", probs.astype(BF16), context_grad).reshape(count, inner).astype(BF16)
        )
        grad_table = mm("hqk,qkb->bh", score_grad, onehot)
        first_part = (
            mm("tc,dc->td", query_grad, w_query)
            + mm("tc,dc->td", key_grad, w_key)
            + mm("tc,dc->td", value_grad, w_value)
        )
        first_part = ready(first_part)
        first_got = mp_other(first_part)
        got_c = swap(ready(sent_part(in_first)), PAIR)
        state_a = line_next(state_a)
        rows_z = finish(state_z)
        qkv_grad = jnp.concatenate([query_grad, key_grad, value_grad], axis=1)
        normed_core = mm("td,dk->tk", normed, core_order).astype(BF16)
        attn_grad_core = mm("td,dk->tk", attn_grad, core_order).astype(BF16)
        _, first_pull = jax.vjp(norm_rows, inputs, gain_one)

        def dense_first(columns):
            return mm("td,tc->dc", normed_core[:, columns], qkv_grad)

        state_b = begin(paired(out_second, got_b), LINE)
        got_d = swap(ready(sent_part(in_second)), PAIR)
        sums_a = core_begin(state_a)
        first_grad = first_part + take(first_got)
        gain_part = ready(first_pull(first_part)[1])
        grad_gain_one = gain_part + take(mp_other(gain_part))
        core_e = swap(ready(dense_first(other)), 1)
        state_b = line_next(state_b)
        own_e = (dense_first(mine) + take(core_e))[None]

        table_rows = jnp.tile(grad_table.reshape(share, -1), (n_dp, 1))
        small = jnp.concatenate(
            [grad_gain_one[:, None], grad_gain_two[:, None], grad_router, table_rows], axis=1
        )
        n_small = small.shape[1]
        small = jnp.pad(small, ((0, 0), (0, -n_small % 128)))
        small = mm("dk,dc->kc", core_order.astype(F32), small, lax.Precision.HIGHEST)

        def dense_second(columns):
            product = mm("td,tc->dc", attn_grad_core[:, columns], context)
            return jnp.concatenate([product, small[columns]], axis=1)

        core_f = swap(ready(dense_second(other)), 1)
        state_c = begin(paired(in_first, got_c), LINE)
        state_e = begin(own_e, 1)
        own_f = (dense_second(mine) + take(core_f))[None]
        expert_got = mp_other(ready(expert_part))
        state_c = line_next(state_c)
        sums_b = core_begin(state_b)
        state_d = begin(paired(in_second, got_d), LINE)
        state_f = begin(own_f, 1)
        state_z = begin(rows_z, 1)
        sums_c = core_begin(state_c)
        state_e = begin(finish(state_e), LINE)
        state_d = line_next(state_d)
        state_f = begin(finish(state_f), LINE)
        expert_full = expert_part + take(expert_got)
        mixed = (middle + gate * expert_full).astype(BF16)
        state_e = line_next(state_e)
        sums_z = core_begin(state_z)
        state_f = line_next(state_f)
        sums_d = core_begin(state_d)
        qkv_sum = finish(state_e)[0]
        last_sum = finish(state_f)[0]
        output_sum = last_sum[:, :inner]
        small = last_sum[:, inner : inner + n_small]
        out_sums = [jnp.concatenate(pair, axis=0) for pair in zip(sums_a, sums_b)]
        in_sums = [jnp.concatenate(three, axis=2) for three in zip(sums_c, sums_d, sums_z)]

        input_grad, _ = first_pull(first_grad)
        grad_tokens = middle_grad + input_grad
        table_total = small[:, 2 + E :].reshape(NB, heads)

        def by_expert(sums):
            mine, other = sums
            first = core == 0
            return jnp.concatenate(
                [jnp.where(first, mine, other), jnp.where(first, other, mine)], axis=0
            )

        return (
            mixed,
            grad_tokens,
            small[:, 0],
            qkv_sum[:, :inner],
            qkv_sum[:, inner : 2 * inner],
            qkv_sum[:, 2 * inner :],
            output_sum.T,
            table_total,
            small[:, 1],
            small[:, 2 : 2 + E],
            by_expert(in_sums),
            jnp.swapaxes(by_expert(out_sums), 1, 2),
        )

    return jax.shard_map(
        shards,
        mesh=mesh,
        in_specs=(
            P("dp", None),
            P(),
            P(None, "mp"),
            P(None, "mp"),
            P(None, "mp"),
            P("mp", None),
            P(None, "mp"),
            P(),
            P(),
            P(None, None, "mp"),
            P(None, "mp", None),
            P("dp", None),
            P("dp", None),
            P("dp"),
        ),
        out_specs=(
            P("dp", None),
            P("dp", None),
            P("dp"),
            P("dp", "mp"),
            P("dp", "mp"),
            P("dp", "mp"),
            P("mp", "dp"),
            P(None, "mp"),
            P("dp"),
            P("dp", None),
            P(None, "dp", "mp"),
            P(None, "mp", "dp"),
        ),
        check_vma=False,
    )
```

```python
import jax
import jax.numpy as jnp
from jax import lax
from jax.experimental import pallas as pl
from jax.experimental.pallas import tpu as pltpu
from jax.sharding import PartitionSpec as P

HEAD = 64
NB = 32
E = 4
CAP = 160
ROWS = 128
CORES = 2
PAIR = 2
LINE = 2
LOCAL = E // CORES

EPS = 1e-06
THRESHOLDS = (12, 16, 23, 32, 46, 64, 91)
F32 = jnp.float32
BF16 = jnp.bfloat16


def segments(lengths, count):
    places = jnp.arange(count, dtype=jnp.int32)
    entry = jnp.arange(lengths.shape[0], dtype=jnp.int32)
    ends = jnp.sum(jnp.where(entry[None, :] <= entry[:, None], lengths[None, :], 0), axis=1)
    return jnp.sum((places[:, None] >= ends[None, :]).astype(jnp.int32), axis=1)


def offset_bucket(offset):
    distance = jnp.abs(offset)
    far_side = 8 + sum(((distance >= edge).astype(jnp.int32) for edge in THRESHOLDS))
    near = jnp.where(distance < 8, distance, far_side)
    return jnp.where(offset > 0, NB // 2, 0) + near


def tile_bias(skewed, index, count):
    start = (2 * count - index * ROWS) % (2 * count)
    if start + count <= 2 * count:
        return skewed[:, start : start + count]
    return jnp.concatenate([skewed[:, start:], skewed[:, : count - (2 * count - start)]], axis=1)


def skew(values, count):
    rows = jnp.broadcast_to(values, (ROWS, 2 * count))
    return pltpu.roll(rows, 0, 1, stride=1, stride_axis=0)


def row_probs(query, keys, bias, allowed):
    scores = lax.dot_general(query, keys, (((1,), (1,)), ((), ())), preferred_element_type=F32)
    scores = jnp.where(allowed, scores + bias, -1000000000.0)
    weights = jnp.exp(scores - jnp.max(scores, axis=1, keepdims=True))
    return weights * (1.0 / jnp.sum(weights, axis=1, keepdims=True))


def attend_kernel(seg_column, seg_row, offsets, query, keys, values, context):
    count = query.shape[0]
    for head in range(2):
        lanes = slice(head * HEAD, (head + 1) * HEAD)
        key, value = keys[:, lanes], values[:, lanes]
        skewed = skew(offsets[0, head : head + 1, :], count)
        for index in range(count // ROWS):
            rows = slice(index * ROWS, (index + 1) * ROWS)
            allowed = seg_column[rows, :] == seg_row[...]
            probs = row_probs(query[rows, lanes], key, tile_bias(skewed, index, count), allowed)
            out = jnp.dot(probs.astype(BF16), value, preferred_element_type=F32)
            context[rows, lanes] = out.astype(BF16)


def attend_back_kernel(
    seg_column, seg_row, offsets, query, keys, values, context_grad, d_query, d_keys, d_values, d_offsets
):
    count = query.shape[0]
    for head in range(2):
        lanes = slice(head * HEAD, (head + 1) * HEAD)
        key, value = keys[:, lanes], values[:, lanes]
        skewed = skew(offsets[0, head : head + 1, :], count)
        key_sum = jnp.zeros((count, HEAD), F32)
        value_sum = jnp.zeros((count, HEAD), F32)
        blocks = 2 * count // ROWS
        diagonal = [jnp.zeros((ROWS, ROWS), F32) for _ in range(blocks)]
        for index in range(count // ROWS):
            rows = slice(index * ROWS, (index + 1) * ROWS)
            allowed = seg_column[rows, :] == seg_row[...]
            row_query, row_grad = query[rows, lanes], context_grad[rows, lanes]
            probs = row_probs(row_query, key, tile_bias(skewed, index, count), allowed)
            prob_grad = lax.dot_general(
                row_grad, value, (((1,), (1,)), ((), ())), preferred_element_type=F32
            )
            centre = jnp.sum(probs * prob_grad, axis=1, keepdims=True)
            score_grad = (probs * (prob_grad - centre)).astype(BF16)
            d_query[rows, lanes] = jnp.dot(score_grad, key, preferred_element_type=F32).astype(BF16)
            turned = (((0,), (0,)), ((), ()))
            key_sum += lax.dot_general(score_grad, row_query, turned, preferred_element_type=F32)
            value_sum += lax.dot_general(
                probs.astype(BF16), row_grad, turned, preferred_element_type=F32
            )
            wide = score_grad.astype(F32)
            for block in range(count // ROWS):
                place = (block - index) % blocks
                diagonal[place] = diagonal[place] + wide[:, block * ROWS : (block + 1) * ROWS]
        d_keys[:, lanes] = key_sum.astype(BF16)
        d_values[:, lanes] = value_sum.astype(BF16)
        skewed_sum = jnp.concatenate(diagonal, axis=1)
        straight = skewed_sum[:8]
        for group in range(8, ROWS, 8):
            straight = straight + pltpu.roll(skewed_sum[group : group + 8], 2 * count - group, 1)
        row = lax.broadcasted_iota(jnp.int32, straight.shape, 0)
        for bit in (1, 2, 4):
            straight = jnp.where(row & bit > 0, pltpu.roll(straight, 2 * count - bit, 1), straight)
        d_offsets[0, head : head + 1, :] = jnp.sum(straight, axis=0, keepdims=True)


def head_pairs(kernel, seg, offsets, arrays, n_out, with_offsets):
    count, inner = arrays[0].shape
    pairs = inner // (2 * HEAD)
    column = pl.BlockSpec((count, 2 * HEAD), lambda i: (0, i))
    line = pl.BlockSpec((1, 2, 2 * count), lambda i: (i, 0, 0))
    out_specs = [column] * n_out + [line] * with_offsets
    out_shape = [jax.ShapeDtypeStruct((count, inner), BF16)] * n_out
    out_shape += [jax.ShapeDtypeStruct((pairs, 2, 2 * count), F32)] * with_offsets
    products = 2 if n_out == 1 else 5
    return pl.pallas_call(
        kernel,
        grid=(pairs,),
        in_specs=[
            pl.BlockSpec((count, 1), lambda i: (0, 0)),
            pl.BlockSpec((1, count), lambda i: (0, 0)),
            line,
            *[column] * len(arrays),
        ],
        out_specs=out_specs,
        out_shape=out_shape,
        cost_estimate=pl.CostEstimate(
            flops=products * 2 * count * count * inner,
            bytes_accessed=2 * count * inner * (len(arrays) + n_out),
            transcendentals=count * count * inner // HEAD,
        ),
        compiler_params=pltpu.CompilerParams(vmem_limit_bytes=32 * 1024 * 1024),
    )(seg[:, None], seg[None, :], offsets, *arrays)


def ranks(expert_ids):
    place = jnp.arange(expert_ids.shape[0], dtype=jnp.int32)
    earlier = (expert_ids[:, None] == expert_ids[None, :]) & (place[None, :] < place[:, None])
    return jnp.sum(earlier.astype(jnp.int32), axis=1)


def norm_rows(values, gain):
    return values * lax.rsqrt(jnp.mean(values * values, axis=-1, keepdims=True) + EPS) * gain


def mm(spec, left, right, precision=None):
    return jnp.einsum(spec, left, right, preferred_element_type=F32, precision=precision)


def solution(mesh):
    n_dp, n_mp = mesh.shape["dp"], mesh.shape["mp"]
    bits = n_dp.bit_length() - 1

    def swap(value, stride):
        return lax.ppermute(value, "dp", [(i, i ^ stride) for i in range(n_dp)])

    def mp_other(value):
        return lax.ppermute(value, "mp", [(0, 1), (1, 0)])

    def shards(
        tokens,
        gain_attn,
        w_query,
        w_key,
        w_value,
        w_output,
        position_table,
        gain_moe,
        w_router,
        w_in,
        w_out,
        cotangent,
        seq_lengths,
        expert_ids,
    ):
        device = lax.axis_index("dp")
        core = device % CORES
        count, width = tokens.shape
        share = width // n_dp
        heads = position_table.shape[1]
        inner = heads * HEAD

        last = []

        def after(value, *deps):
            return lax.optimization_barrier((value, *deps))[0] if deps else value

        def ready(value):
            value = after(value, *last)
            last[:] = [value]
            return value

        def take(got):
            got = after(got, *last)
            last[:] = [got]
            return got

        def begin(rows, bit):
            half = rows.shape[1] // 2
            return rows[:, half:], swap(ready(rows[:, :half]), 1 << bit)

        def finish(state):
            kept, got = state
            return kept + take(got)

        def line_next(state):
            for bit in range(LINE + 1, bits - 1):
                state = begin(finish(state), bit)
            return begin(finish(state), bits - 1)

        def core_begin(state):
            return begin(finish(state), 0)

        feature = jnp.arange(width, dtype=jnp.int32)
        half_width = width // 2

        def column_order(names):
            source = feature % share
            for place, name in enumerate(names):
                same = (feature // share) >> (bits - 1 - place) & 1
                bit = (device >> name & 1) ^ (1 - same)
                source = source + (bit << name) * share
            return (feature[:, None] == source[None, :]).astype(BF16)

        line_bits = list(range(LINE, bits))
        pair_order = column_order([1, *line_bits, 0])
        line_order = column_order([*line_bits, 1, 0])
        core_order = column_order([0, 1, *line_bits])

        segment = segments(seq_lengths[0], count)
        inputs = tokens.astype(F32)
        gain_one = gain_attn.astype(F32)
        gain_two = gain_moe.astype(F32)
        bucket_ids = jnp.arange(NB, dtype=jnp.int32)
        normed = norm_rows(inputs, gain_one).astype(BF16)
        query = mm("td,dc->tc", normed, w_query).astype(BF16)
        keys = mm("td,dc->tc", normed, w_key).astype(BF16)
        values = mm("td,dc->tc", normed, w_value).astype(BF16)

        place = jnp.arange(2 * count, dtype=jnp.int32)
        bucket = offset_bucket(jnp.where(place < count, place, place - 2 * count))
        onehot = (bucket[:, None] == bucket_ids[None, :]).astype(F32)
        offsets = mm("ob,bh->ho", onehot, position_table.astype(F32), lax.Precision.HIGHEST)
        offsets = offsets.reshape(heads // 2, 2, 2 * count)
        (context,) = head_pairs(attend_kernel, segment, offsets, [query, keys, values], 1, 0)
        attended = mm("tc,cd->td", context, w_output)
        attended_got = mp_other(attended)

        rank = ranks(expert_ids)
        local = (expert_ids - LOCAL * core) % E
        slot = jnp.where(rank < CAP, local * CAP + rank, -1)
        select = jnp.arange(E * CAP, dtype=jnp.int32)[:, None] == slot[None, :]
        select_low = select.astype(BF16)
        select_full = select.astype(F32)
        picked = (expert_ids[:, None] == jnp.arange(E, dtype=jnp.int32)[None, :]).astype(F32)
        my_in = lax.dynamic_slice_in_dim(w_in, LOCAL * core, LOCAL, 0)
        my_out = lax.dynamic_slice_in_dim(w_out, LOCAL * core, LOCAL, 0)

        half = LOCAL * CAP

        def to_experts(rows):
            slots = mm("st,td->sd", select_low, rows)
            return slots[:half], swap(slots[half:], 1)

        def scaled(parts, weight):
            both = [
                (part * scale[:, None]).reshape(LOCAL, CAP, width)
                for part, scale in zip(parts, weight)
            ]
            return jnp.concatenate(both, axis=1).astype(BF16)

        def slot_values(values):
            slots = jnp.sum(jnp.where(select, values[None, :], 0.0), axis=1)
            return slots[:half], swap(slots[half:], 1)

        live = slot_values(jnp.ones((count,), F32))
        seed_slots = to_experts(cotangent)

        def to_tokens(slots):
            got = swap(slots[:, CAP:], 1)
            both = jnp.concatenate([slots[:, :CAP], got], axis=0).reshape(E * CAP, width)
            return mm("st,sd->td", select_full, both, lax.Precision.HIGH)

        normed_core = mm("td,dk->tk", normed, core_order).astype(BF16)
        attended_got, my_in, my_out, seed_slots, live, normed_core = lax.optimization_barrier(
            (attended_got, my_in, my_out, seed_slots, live, normed_core)
        )
        middle = inputs + (attended + attended_got)
        normed_two = norm_rows(middle, gain_two).astype(BF16)
        dispatch = scaled(to_experts(normed_two), live)
        logits = mm("td,de->te", normed_two, w_router)
        router = jax.nn.softmax(logits, axis=-1)
        gate = jnp.sum(router * picked, axis=1, keepdims=True)
        grad_seed = cotangent.astype(F32)
        slot_grad = scaled(seed_slots, slot_values(gate[:, 0]))

        pre_act = mm("ecd,edf->ecf", dispatch, my_in)
        hidden, gelu_pull = jax.vjp(jax.nn.gelu, pre_act)
        hidden = hidden.astype(BF16)
        units = hidden.shape[2]
        slot_grad_pair = mm("ecd,dk->eck", slot_grad, pair_order).astype(BF16)

        def grads(left, right):
            return mm("ecd,ecf->edf", left, right)

        def paired(pair, got):
            return grads(pair[0][:, :, mine], pair[1]) + take(got)

        out_first = slot_grad_pair[:1], hidden[:1]
        out_second = slot_grad_pair[1:], hidden[1:]
        other, mine = slice(0, half_width), slice(half_width, width)

        def sent_part(pair):
            return grads(pair[0][:, :, other], pair[1])

        got_a = swap(ready(sent_part(out_first)), PAIR)
        hidden_grad = mm("ecd,efd->ecf", after(slot_grad, *last), my_out)
        pre_grad = gelu_pull(hidden_grad)[0].astype(BF16)
        back_slots = mm("ecf,edf->ecd", pre_grad, my_in)
        part_slots = mm("ecf,efd->ecd", after(hidden, *last), my_out)
        cut_at = units * 2 // 3
        dispatch_pair = mm("ecd,dk->eck", dispatch, pair_order).astype(BF16)
        dispatch_line = mm("ecd,dk->eck", dispatch, line_order).astype(BF16)
        in_first = dispatch_pair, pre_grad[:, :, : cut_at // 2]
        in_second = dispatch_pair, pre_grad[:, :, cut_at // 2 : cut_at]
        in_third = dispatch_line, pre_grad[:, :, cut_at:]
        expert_part = to_tokens(part_slots)
        back_part = to_tokens(back_slots)
        state_z = None, swap(ready(sent_part(in_third)), 1 << LINE)
        gate_part = jnp.sum(grad_seed * expert_part, axis=1)
        gate_rows = jnp.pad(gate_part.reshape(-1, count // 4), ((0, 4), (0, width - count // 4)))
        back = ready(jnp.concatenate([back_part, gate_rows], axis=0))
        back_got = mp_other(back)
        got_b = swap(ready(sent_part(out_second)), PAIR)
        state_z = line_next((grads(in_third[0][:, :, mine], in_third[1]), state_z[1]))
        state_a = begin(paired(out_first, got_a), LINE)
        back_sum = back + take(back_got)
        expert_back = back_sum[:count]
        gate_grad = back_sum[count : count + 4, : count // 4].reshape(count, 1)

        logit_grad = (gate_grad * gate * (picked - router)).astype(BF16)
        grad_router = mm("td,te->de", normed_two, logit_grad)
        second_grad = expert_back + mm("te,de->td", logit_grad, w_router)
        _, second_pull = jax.vjp(norm_rows, middle, gain_two)
        middle_grad, grad_gain_two = second_pull(second_grad)
        middle_grad = middle_grad + grad_seed
        attn_grad = middle_grad.astype(BF16)
        context_grad = mm("td,cd->tc", attn_grad, w_output).astype(BF16)
        query_grad, key_grad, value_grad, offset_grad = head_pairs(
            attend_back_kernel,
            segment,
            offsets,
            [query, keys, values, context_grad],
            3,
            1,
        )
        offset_grad = offset_grad.reshape(heads, 2 * count)
        grad_table = mm("ho,ob->bh", offset_grad, onehot, lax.Precision.HIGHEST)
        first_part = (
            mm("tc,dc->td", query_grad, w_query)
            + mm("tc,dc->td", key_grad, w_key)
            + mm("tc,dc->td", value_grad, w_value)
        )
        _, first_pull = jax.vjp(norm_rows, inputs, gain_one)
        gain_rows = jnp.pad(first_pull(first_part)[1][None], ((0, 7), (0, 0)))
        first_rows = ready(jnp.concatenate([first_part, gain_rows], axis=0))
        first_got = mp_other(first_rows)
        got_c = swap(ready(sent_part(in_first)), PAIR)
        state_a = line_next(state_a)
        rows_z = finish(state_z)
        state_b = begin(paired(out_second, got_b), LINE)
        got_d = swap(ready(sent_part(in_second)), PAIR)
        sums_a = core_begin(state_a)
        first_got = take(first_got)
        state_b = line_next(state_b)
        state_c = begin(paired(in_first, got_c), LINE)
        first_rows = first_rows + after(first_got, *last)
        first_grad = first_rows[:count]
        grad_gain_one = first_rows[count]
        qkv_grad = after(jnp.concatenate([query_grad, key_grad, value_grad], axis=1), *last)
        attn_grad_core = mm("td,dk->tk", attn_grad, core_order).astype(BF16)

        def dense_first(columns):
            return mm("td,tc->dc", normed_core[:, columns], qkv_grad)

        core_e = swap(ready(dense_first(other)), 1)
        sums_b = core_begin(state_b)
        own_e = (dense_first(mine) + take(core_e))[None]
        state_e = begin(own_e, 1)

        table_rows = jnp.tile(grad_table.reshape(share, -1), (n_dp, 1))
        small = jnp.concatenate(
            [grad_gain_one[:, None], grad_gain_two[:, None], grad_router, table_rows], axis=1
        )
        n_small = small.shape[1]
        small = jnp.pad(small, ((0, 0), (0, -n_small % 128)))
        small = mm("dk,dc->kc", core_order.astype(F32), small, lax.Precision.HIGHEST)

        def dense_second(columns):
            product = mm("td,tc->dc", attn_grad_core[:, columns], context)
            return jnp.concatenate([product, small[columns]], axis=1)

        core_f = swap(ready(dense_second(other)), 1)
        state_c = line_next(state_c)
        own_f = (dense_second(mine) + take(core_f))[None]
        state_d = begin(paired(in_second, got_d), LINE)
        state_f = begin(own_f, 1)
        state_z = begin(rows_z, 1)
        sums_c = core_begin(state_c)
        expert_got = mp_other(ready(expert_part))
        state_e = begin(finish(state_e), LINE)
        state_f = begin(finish(state_f), LINE)
        state_d = line_next(state_d)
        sums_z = core_begin(state_z)
        state_e = line_next(state_e)
        state_f = line_next(state_f)
        sums_d = core_begin(state_d)
        expert_full = expert_part + take(expert_got)
        mixed = (middle + gate * expert_full).astype(BF16)
        qkv_sum = finish(state_e)[0]
        last_sum = finish(state_f)[0]
        output_sum = last_sum[:, :inner]
        small = last_sum[:, inner : inner + n_small]
        out_sums = [jnp.concatenate(pair, axis=0) for pair in zip(sums_a, sums_b)]
        in_sums = [jnp.concatenate(three, axis=2) for three in zip(sums_c, sums_d, sums_z)]

        input_grad, _ = first_pull(first_grad)
        grad_tokens = middle_grad + input_grad
        table_total = small[:, 2 + E :].reshape(NB, heads)

        def by_expert(sums):
            mine, other = sums
            first = core == 0
            return jnp.concatenate(
                [jnp.where(first, mine, other), jnp.where(first, other, mine)], axis=0
            )

        return (
            mixed,
            grad_tokens,
            small[:, 0],
            qkv_sum[:, :inner],
            qkv_sum[:, inner : 2 * inner],
            qkv_sum[:, 2 * inner :],
            output_sum.T,
            table_total,
            small[:, 1],
            small[:, 2 : 2 + E],
            by_expert(in_sums),
            jnp.swapaxes(by_expert(out_sums), 1, 2),
        )

    return jax.shard_map(
        shards,
        mesh=mesh,
        in_specs=(
            P("dp", None),
            P(),
            P(None, "mp"),
            P(None, "mp"),
            P(None, "mp"),
            P("mp", None),
            P(None, "mp"),
            P(),
            P(),
            P(None, None, "mp"),
            P(None, "mp", None),
            P("dp", None),
            P("dp", None),
            P("dp"),
        ),
        out_specs=(
            P("dp", None),
            P("dp", None),
            P("dp"),
            P("dp", "mp"),
            P("dp", "mp"),
            P("dp", "mp"),
            P("mp", "dp"),
            P(None, "mp"),
            P("dp"),
            P("dp", None),
            P(None, "dp", "mp"),
            P(None, "mp", "dp"),
        ),
        check_vma=False,
    )
```

```python
import jax
import jax.numpy as jnp
from jax import lax
from jax.experimental import pallas as pl
from jax.experimental.pallas import tpu as pltpu
from jax.sharding import PartitionSpec as P

HEAD = 64
NB = 32
E = 4
CAP = 160
ROWS = 128
CORES = 2
PAIR = 2
LINE = 2
LOCAL = E // CORES

EPS = 1e-06
THRESHOLDS = (12, 16, 23, 32, 46, 64, 91)
F32 = jnp.float32
BF16 = jnp.bfloat16


def segments(lengths, count):
    places = jnp.arange(count, dtype=jnp.int32)
    entry = jnp.arange(lengths.shape[0], dtype=jnp.int32)
    ends = jnp.sum(jnp.where(entry[None, :] <= entry[:, None], lengths[None, :], 0), axis=1)
    return jnp.sum((places[:, None] >= ends[None, :]).astype(jnp.int32), axis=1)


def offset_bucket(offset):
    distance = jnp.abs(offset)
    far_side = 8 + sum(((distance >= edge).astype(jnp.int32) for edge in THRESHOLDS))
    near = jnp.where(distance < 8, distance, far_side)
    return jnp.where(offset > 0, NB // 2, 0) + near


def tile_bias(skewed, index, count):
    start = (2 * count - index * ROWS) % (2 * count)
    if start + count <= 2 * count:
        return skewed[:, start : start + count]
    return jnp.concatenate([skewed[:, start:], skewed[:, : count - (2 * count - start)]], axis=1)


def skew(values, count):
    rows = jnp.broadcast_to(values, (ROWS, 2 * count))
    return pltpu.roll(rows, 0, 1, stride=1, stride_axis=0)


def row_probs(query, keys, bias, allowed):
    scores = lax.dot_general(query, keys, (((1,), (1,)), ((), ())), preferred_element_type=F32)
    scores = jnp.where(allowed, scores + bias, -1000000000.0)
    weights = jnp.exp(scores - jnp.max(scores, axis=1, keepdims=True))
    return weights * (1.0 / jnp.sum(weights, axis=1, keepdims=True))


def attend_kernel(seg_column, seg_row, offsets, query, keys, values, context):
    count = query.shape[0]
    for head in range(2):
        lanes = slice(head * HEAD, (head + 1) * HEAD)
        key, value = keys[:, lanes], values[:, lanes]
        skewed = skew(offsets[0, head : head + 1, :], count)
        for index in range(count // ROWS):
            rows = slice(index * ROWS, (index + 1) * ROWS)
            allowed = seg_column[rows, :] == seg_row[...]
            probs = row_probs(query[rows, lanes], key, tile_bias(skewed, index, count), allowed)
            out = jnp.dot(probs.astype(BF16), value, preferred_element_type=F32)
            context[rows, lanes] = out.astype(BF16)


def attend_back_kernel(
    seg_column, seg_row, offsets, query, keys, values, context_grad, d_query, d_keys, d_values, d_offsets
):
    count = query.shape[0]
    for head in range(2):
        lanes = slice(head * HEAD, (head + 1) * HEAD)
        key, value = keys[:, lanes], values[:, lanes]
        skewed = skew(offsets[0, head : head + 1, :], count)
        key_sum = jnp.zeros((count, HEAD), F32)
        value_sum = jnp.zeros((count, HEAD), F32)
        blocks = 2 * count // ROWS
        diagonal = [jnp.zeros((ROWS, ROWS), F32) for _ in range(blocks)]
        for index in range(count // ROWS):
            rows = slice(index * ROWS, (index + 1) * ROWS)
            allowed = seg_column[rows, :] == seg_row[...]
            row_query, row_grad = query[rows, lanes], context_grad[rows, lanes]
            probs = row_probs(row_query, key, tile_bias(skewed, index, count), allowed)
            prob_grad = lax.dot_general(
                row_grad, value, (((1,), (1,)), ((), ())), preferred_element_type=F32
            )
            centre = jnp.sum(probs * prob_grad, axis=1, keepdims=True)
            score_grad = (probs * (prob_grad - centre)).astype(BF16)
            d_query[rows, lanes] = jnp.dot(score_grad, key, preferred_element_type=F32).astype(BF16)
            turned = (((0,), (0,)), ((), ()))
            key_sum += lax.dot_general(score_grad, row_query, turned, preferred_element_type=F32)
            value_sum += lax.dot_general(
                probs.astype(BF16), row_grad, turned, preferred_element_type=F32
            )
            wide = score_grad.astype(F32)
            for block in range(count // ROWS):
                place = (block - index) % blocks
                diagonal[place] = diagonal[place] + wide[:, block * ROWS : (block + 1) * ROWS]
        d_keys[:, lanes] = key_sum.astype(BF16)
        d_values[:, lanes] = value_sum.astype(BF16)
        skewed_sum = jnp.concatenate(diagonal, axis=1)
        straight = skewed_sum[:8]
        for group in range(8, ROWS, 8):
            straight = straight + pltpu.roll(skewed_sum[group : group + 8], 2 * count - group, 1)
        row = lax.broadcasted_iota(jnp.int32, straight.shape, 0)
        for bit in (1, 2, 4):
            straight = jnp.where(row & bit > 0, pltpu.roll(straight, 2 * count - bit, 1), straight)
        d_offsets[0, head : head + 1, :] = jnp.sum(straight, axis=0, keepdims=True)


def head_pairs(kernel, seg, offsets, arrays, n_out, with_offsets):
    count, inner = arrays[0].shape
    pairs = inner // (2 * HEAD)
    column = pl.BlockSpec((count, 2 * HEAD), lambda i: (0, i))
    line = pl.BlockSpec((1, 2, 2 * count), lambda i: (i, 0, 0))
    out_specs = [column] * n_out + [line] * with_offsets
    out_shape = [jax.ShapeDtypeStruct((count, inner), BF16)] * n_out
    out_shape += [jax.ShapeDtypeStruct((pairs, 2, 2 * count), F32)] * with_offsets
    products = 2 if n_out == 1 else 5
    return pl.pallas_call(
        kernel,
        grid=(pairs,),
        in_specs=[
            pl.BlockSpec((count, 1), lambda i: (0, 0)),
            pl.BlockSpec((1, count), lambda i: (0, 0)),
            line,
            *[column] * len(arrays),
        ],
        out_specs=out_specs,
        out_shape=out_shape,
        cost_estimate=pl.CostEstimate(
            flops=products * 2 * count * count * inner,
            bytes_accessed=2 * count * inner * (len(arrays) + n_out),
            transcendentals=count * count * inner // HEAD,
        ),
        compiler_params=pltpu.CompilerParams(vmem_limit_bytes=32 * 1024 * 1024),
    )(seg[:, None], seg[None, :], offsets, *arrays)


def ranks(expert_ids):
    place = jnp.arange(expert_ids.shape[0], dtype=jnp.int32)
    earlier = (expert_ids[:, None] == expert_ids[None, :]) & (place[None, :] < place[:, None])
    return jnp.sum(earlier.astype(jnp.int32), axis=1)


def norm_rows(values, gain):
    return values * lax.rsqrt(jnp.mean(values * values, axis=-1, keepdims=True) + EPS) * gain


def mm(spec, left, right, precision=None):
    return jnp.einsum(spec, left, right, preferred_element_type=F32, precision=precision)


def solution(mesh):
    n_dp, n_mp = mesh.shape["dp"], mesh.shape["mp"]
    bits = n_dp.bit_length() - 1

    def swap(value, stride):
        return lax.ppermute(value, "dp", [(i, i ^ stride) for i in range(n_dp)])

    def mp_other(value):
        return lax.ppermute(value, "mp", [(0, 1), (1, 0)])

    def shards(
        tokens,
        gain_attn,
        w_query,
        w_key,
        w_value,
        w_output,
        position_table,
        gain_moe,
        w_router,
        w_in,
        w_out,
        cotangent,
        seq_lengths,
        expert_ids,
    ):
        device = lax.axis_index("dp")
        core = device % CORES
        count, width = tokens.shape
        share = width // n_dp
        heads = position_table.shape[1]
        inner = heads * HEAD

        last = []

        def after(value, *deps):
            return lax.optimization_barrier((value, *deps))[0] if deps else value

        def ready(value):
            value = after(value, *last)
            last[:] = [value]
            return value

        def take(got):
            got = after(got, *last)
            last[:] = [got]
            return got

        def begin(rows, bit):
            half = rows.shape[1] // 2
            return rows[:, half:], swap(ready(rows[:, :half]), 1 << bit)

        def finish(state):
            kept, got = state
            return kept + take(got)

        def line_next(state):
            for bit in range(LINE + 1, bits - 1):
                state = begin(finish(state), bit)
            return begin(finish(state), bits - 1)

        def core_begin(state):
            return begin(finish(state), 0)

        feature = jnp.arange(width, dtype=jnp.int32)
        half_width = width // 2

        def column_order(names):
            source = feature % share
            for place, name in enumerate(names):
                same = (feature // share) >> (bits - 1 - place) & 1
                bit = (device >> name & 1) ^ (1 - same)
                source = source + (bit << name) * share
            return (feature[:, None] == source[None, :]).astype(BF16)

        line_bits = list(range(LINE, bits))
        pair_order = column_order([1, *line_bits, 0])
        line_order = column_order([*line_bits, 1, 0])
        core_order = column_order([0, 1, *line_bits])

        segment = segments(seq_lengths[0], count)
        inputs = tokens.astype(F32)
        gain_one = gain_attn.astype(F32)
        gain_two = gain_moe.astype(F32)
        bucket_ids = jnp.arange(NB, dtype=jnp.int32)
        normed = norm_rows(inputs, gain_one).astype(BF16)
        query = mm("td,dc->tc", normed, w_query).astype(BF16)
        keys = mm("td,dc->tc", normed, w_key).astype(BF16)
        values = mm("td,dc->tc", normed, w_value).astype(BF16)

        place = jnp.arange(2 * count, dtype=jnp.int32)
        bucket = offset_bucket(jnp.where(place < count, place, place - 2 * count))
        onehot = (bucket[:, None] == bucket_ids[None, :]).astype(F32)
        offsets = mm("ob,bh->ho", onehot, position_table.astype(F32), lax.Precision.HIGHEST)
        offsets = offsets.reshape(heads // 2, 2, 2 * count)
        (context,) = head_pairs(attend_kernel, segment, offsets, [query, keys, values], 1, 0)
        attended = mm("tc,cd->td", context, w_output)
        attended_got = mp_other(attended)

        rank = ranks(expert_ids)
        local = (expert_ids - LOCAL * core) % E
        slot = jnp.where(rank < CAP, local * CAP + rank, -1)
        select = jnp.arange(E * CAP, dtype=jnp.int32)[:, None] == slot[None, :]
        select_low = select.astype(BF16)
        select_full = select.astype(F32)
        picked = (expert_ids[:, None] == jnp.arange(E, dtype=jnp.int32)[None, :]).astype(F32)
        my_in = lax.dynamic_slice_in_dim(w_in, LOCAL * core, LOCAL, 0)
        my_out = lax.dynamic_slice_in_dim(w_out, LOCAL * core, LOCAL, 0)

        half = LOCAL * CAP

        def to_experts(rows):
            slots = mm("st,td->sd", select_low, rows)
            return slots[:half], swap(slots[half:], 1)

        def scaled(parts, weight):
            both = [
                (part * scale[:, None]).reshape(LOCAL, CAP, width)
                for part, scale in zip(parts, weight)
            ]
            return jnp.concatenate(both, axis=1).astype(BF16)

        def slot_values(values):
            slots = jnp.sum(jnp.where(select, values[None, :], 0.0), axis=1)
            return slots[:half], swap(slots[half:], 1)

        live = slot_values(jnp.ones((count,), F32))
        seed_slots = to_experts(cotangent)

        def to_tokens(slots):
            got = swap(slots[:, CAP:], 1)
            both = jnp.concatenate([slots[:, :CAP], got], axis=0).reshape(E * CAP, width)
            return mm("st,sd->td", select_full, both, lax.Precision.HIGH)

        normed_core = mm("td,dk->tk", normed, core_order).astype(BF16)
        attended_got, my_in, my_out, seed_slots, live, normed_core = lax.optimization_barrier(
            (attended_got, my_in, my_out, seed_slots, live, normed_core)
        )
        middle = inputs + (attended + attended_got)
        normed_two = norm_rows(middle, gain_two).astype(BF16)
        dispatch = scaled(to_experts(normed_two), live)
        logits = mm("td,de->te", normed_two, w_router)
        router = jax.nn.softmax(logits, axis=-1)
        gate = jnp.sum(router * picked, axis=1, keepdims=True)
        grad_seed = cotangent.astype(F32)
        slot_grad = scaled(seed_slots, slot_values(gate[:, 0]))

        pre_act = mm("ecd,edf->ecf", dispatch, my_in)
        hidden, gelu_pull = jax.vjp(jax.nn.gelu, pre_act)
        hidden = hidden.astype(BF16)
        units = hidden.shape[2]
        slot_grad_pair = mm("ecd,dk->eck", slot_grad, pair_order).astype(BF16)

        def grads(left, right):
            return mm("ecd,ecf->edf", left, right)

        def paired(pair, got):
            return grads(pair[0][:, :, mine], pair[1]) + take(got)

        out_first = slot_grad_pair[:1], hidden[:1]
        out_second = slot_grad_pair[1:], hidden[1:]
        other, mine = slice(0, half_width), slice(half_width, width)

        def sent_part(pair):
            return grads(pair[0][:, :, other], pair[1])

        got_a = swap(ready(sent_part(out_first)), PAIR)
        hidden_grad = mm("ecd,efd->ecf", after(slot_grad, *last), my_out)
        pre_grad = gelu_pull(hidden_grad)[0].astype(BF16)
        back_slots = mm("ecf,edf->ecd", pre_grad, my_in)
        part_slots = mm("ecf,efd->ecd", after(hidden, *last), my_out)
        cut_at = units * 2 // 3
        dispatch_pair = mm("ecd,dk->eck", dispatch, pair_order).astype(BF16)
        dispatch_line = mm("ecd,dk->eck", dispatch, line_order).astype(BF16)
        in_first = dispatch_pair, pre_grad[:, :, : cut_at // 2]
        in_second = dispatch_pair, pre_grad[:, :, cut_at // 2 : cut_at]
        in_third = dispatch_line, pre_grad[:, :, cut_at:]
        expert_part = to_tokens(part_slots)
        back_part = to_tokens(back_slots)
        state_z = None, swap(ready(sent_part(in_third)), 1 << LINE)
        gate_part = jnp.sum(grad_seed * expert_part, axis=1)
        gate_rows = jnp.pad(gate_part.reshape(-1, count // 4), ((0, 4), (0, width - count // 4)))
        back = ready(jnp.concatenate([back_part, gate_rows], axis=0))
        back_got = mp_other(back)
        got_b = swap(ready(sent_part(out_second)), PAIR)
        state_z = line_next((grads(in_third[0][:, :, mine], in_third[1]), state_z[1]))
        state_a = begin(paired(out_first, got_a), LINE)
        back_sum = back + take(back_got)
        expert_back = back_sum[:count]
        gate_grad = back_sum[count : count + 4, : count // 4].reshape(count, 1)

        logit_grad = (gate_grad * gate * (picked - router)).astype(BF16)
        grad_router = mm("td,te->de", normed_two, logit_grad)
        second_grad = expert_back + mm("te,de->td", logit_grad, w_router)
        _, second_pull = jax.vjp(norm_rows, middle, gain_two)
        middle_grad, grad_gain_two = second_pull(second_grad)
        middle_grad = middle_grad + grad_seed
        attn_grad = middle_grad.astype(BF16)
        context_grad = mm("td,cd->tc", attn_grad, w_output).astype(BF16)
        query_grad, key_grad, value_grad, offset_grad = head_pairs(
            attend_back_kernel,
            segment,
            offsets,
            [query, keys, values, context_grad],
            3,
            1,
        )
        offset_grad = offset_grad.reshape(heads, 2 * count)
        grad_table = mm("ho,ob->bh", offset_grad, onehot, lax.Precision.HIGHEST)
        first_part = (
            mm("tc,dc->td", query_grad, w_query)
            + mm("tc,dc->td", key_grad, w_key)
            + mm("tc,dc->td", value_grad, w_value)
        )
        _, first_pull = jax.vjp(norm_rows, inputs, gain_one)
        gain_rows = jnp.pad(first_pull(first_part)[1][None], ((0, 7), (0, 0)))
        first_rows = ready(jnp.concatenate([first_part, gain_rows], axis=0))
        first_got = mp_other(first_rows)
        got_c = swap(ready(sent_part(in_first)), PAIR)
        state_a = line_next(state_a)
        rows_z = finish(state_z)
        state_b = begin(paired(out_second, got_b), LINE)
        got_d = swap(ready(sent_part(in_second)), PAIR)
        sums_a = core_begin(state_a)
        first_got = take(first_got)
        state_b = line_next(state_b)
        state_c = begin(paired(in_first, got_c), LINE)
        first_rows = first_rows + after(first_got, *last)
        first_grad = first_rows[:count]
        grad_gain_one = first_rows[count]
        qkv_grad = after(jnp.concatenate([query_grad, key_grad, value_grad], axis=1), *last)
        attn_grad_core = mm("td,dk->tk", attn_grad, core_order).astype(BF16)

        def dense_first(columns):
            return mm("td,tc->dc", normed_core[:, columns], qkv_grad)

        core_e = swap(ready(dense_first(other)), 1)
        sums_b = core_begin(state_b)
        own_e = (dense_first(mine) + take(core_e))[None]
        state_e = begin(own_e, 1)

        table_rows = jnp.tile(grad_table.reshape(share, -1), (n_dp, 1))
        small = jnp.concatenate(
            [grad_gain_one[:, None], grad_gain_two[:, None], grad_router, table_rows], axis=1
        )
        n_small = small.shape[1]
        small = jnp.pad(small, ((0, 0), (0, -n_small % 128)))
        small = mm("dk,dc->kc", core_order.astype(F32), small, lax.Precision.HIGHEST)

        def dense_second(columns):
            product = mm("td,tc->dc", attn_grad_core[:, columns], context)
            return jnp.concatenate([product, small[columns]], axis=1)

        core_f = swap(ready(dense_second(other)), 1)
        state_c = line_next(state_c)
        own_f = (dense_second(mine) + take(core_f))[None]
        state_d = begin(paired(in_second, got_d), LINE)
        state_f = begin(own_f, 1)
        state_z = begin(rows_z, 1)
        sums_c = core_begin(state_c)
        expert_got = mp_other(ready(expert_part))
        state_e = begin(finish(state_e), LINE)
        state_f = begin(finish(state_f), LINE)
        state_d = line_next(state_d)
        state_e = line_next(state_e)
        sums_z = core_begin(state_z)
        state_f = line_next(state_f)
        qkv_sum = finish(state_e)[0]
        last_sum = finish(state_f)[0]
        sums_d = core_begin(state_d)
        expert_full = expert_part + take(expert_got)
        mixed = (middle + gate * expert_full).astype(BF16)
        output_sum = last_sum[:, :inner]
        small = last_sum[:, inner : inner + n_small]
        out_sums = [jnp.concatenate(pair, axis=0) for pair in zip(sums_a, sums_b)]
        in_sums = [jnp.concatenate(three, axis=2) for three in zip(sums_c, sums_d, sums_z)]

        input_grad, _ = first_pull(first_grad)
        grad_tokens = middle_grad + input_grad
        table_total = small[:, 2 + E :].reshape(NB, heads)

        def by_expert(sums):
            mine, other = sums
            first = core == 0
            return jnp.concatenate(
                [jnp.where(first, mine, other), jnp.where(first, other, mine)], axis=0
            )

        return (
            mixed,
            grad_tokens,
            small[:, 0],
            qkv_sum[:, :inner],
            qkv_sum[:, inner : 2 * inner],
            qkv_sum[:, 2 * inner :],
            output_sum.T,
            table_total,
            small[:, 1],
            small[:, 2 : 2 + E],
            by_expert(in_sums),
            jnp.swapaxes(by_expert(out_sums), 1, 2),
        )

    return jax.shard_map(
        shards,
        mesh=mesh,
        in_specs=(
            P("dp", None),
            P(),
            P(None, "mp"),
            P(None, "mp"),
            P(None, "mp"),
            P("mp", None),
            P(None, "mp"),
            P(),
            P(),
            P(None, None, "mp"),
            P(None, "mp", None),
            P("dp", None),
            P("dp", None),
            P("dp"),
        ),
        out_specs=(
            P("dp", None),
            P("dp", None),
            P("dp"),
            P("dp", "mp"),
            P("dp", "mp"),
            P("dp", "mp"),
            P("mp", "dp"),
            P(None, "mp"),
            P("dp"),
            P("dp", None),
            P(None, "dp", "mp"),
            P(None, "mp", "dp"),
        ),
        check_vma=False,
    )
```
